128 devices in a mesh: grp: 16 (over y_hi, z, core), tp: 8 (over y_lo, x).
Axes of the slice: x: 4, y: 4 (y_hi: 2, y_lo: 2; y = y_hi * 2 + y_lo), z: 4, core: 2. Of those that a mesh axis runs over, the one named last changes fastest.
Arguments:
- hidden: bfloat16 [1024, 5120], P('grp', 'tp'), may hold values from -8 to 8
- query_key_value_weight: bfloat16 [5120, 10240], P(('grp', 'tp')), as said below
- w_out: bfloat16 [8192, 5120], P(None, ('grp', 'tp')), may hold values from -0.0625 to 0.0625
- k_cache: bfloat16 [128, 4096, 8, 128], P('grp', None, 'tp'), may hold values from -256 to 256
- value_cache: bfloat16 [128, 4096, 8, 128], P('grp', None, 'tp'), may hold values from -6 to 6
- lengths: int32 [1024], P('grp'), may hold values from 1 to 4096, as said below
- assign: int32 [1024], P('grp'), may hold values from 0 to 7, as said below
Outputs:
- attended: bfloat16 [1024, 5120], P('grp', 'tp')
The draws below stay inside these ranges and needn't reach their ends.
Inputs may be any that keep to these rules, and one draw needn't show every extreme that they name: `lengths`: some row has length 4096. `assign`: within each rollout group's 64 rows every prompt is named by exactly 8 rows. `query_key_value_weight`: entries lie within 6 / sqrt(5120) of zero.
All inputs are finite; a program needn't handle non-finite values.
Results may differ from the reference program's by a relative error of at most 0.007.
Values may be sent and summed in bfloat16 or wider, within the bound.
A program may use at most 192 MiB of HBM per device.

```python
import jax
import jax.numpy as jnp
from jax import lax

D = 5120
QUERY_HEADS = 64
KEY_VALUE_HEADS = 8
HEAD_SIZE = 128
CONTEXT_SLOTS = 4096
SAMPLE_COUNT = 8
PROMPTS = 8
QUERY_PER_KEY = 8
ROWS_GRP = 64
ROW_TOTAL = 1024
PROMPT_TOTAL = 128
QKV = 10240


def draw_hidden(key, part):
    key = jax.random.fold_in(key, 5)
    noise_random_key = jax.random.fold_in(key, 0)
    entry_list = jnp.clip(jax.random.normal(noise_random_key, (ROW_TOTAL, D), jnp.float32), -6.0, 6.0)
    return entry_list.astype(jnp.bfloat16)


def draw_query_key_value_weight(key, part):
    key = jax.random.fold_in(key, 7)
    noise_random_key = jax.random.fold_in(key, 0)
    entry_list = jnp.clip(jax.random.normal(noise_random_key, (D, QKV), jnp.float32), -6.0, 6.0)
    return (entry_list * D ** (-0.5)).astype(jnp.bfloat16)


def draw_k_cache(key, part):
    key = jax.random.fold_in(key, 13)
    noise_random_key = jax.random.fold_in(key, 0)
    entry_list = jnp.clip(jax.random.normal(noise_random_key, (PROMPT_TOTAL, CONTEXT_SLOTS, KEY_VALUE_HEADS, HEAD_SIZE), jnp.float32), -6.0, 6.0)
    return entry_list.astype(jnp.bfloat16)


def draw_lengths(key, part):
    key = jax.random.fold_in(key, 11)
    lens = jax.random.randint(key, (ROW_TOTAL,), 1, CONTEXT_SLOTS + 1)
    return lens.at[0].set(CONTEXT_SLOTS).astype(jnp.int32)


def draw_assign(key, part):
    key = jax.random.fold_in(key, 23)
    keys = jax.random.split(key, ROW_TOTAL // ROWS_GRP)

    def shuffled(sub_key):
        return jax.random.permutation(sub_key, ROWS_GRP)
    perms = jax.vmap(shuffled)(keys)
    return (perms // SAMPLE_COUNT).reshape(ROW_TOTAL).astype(jnp.int32)


def level_of(key, extent, cuts, least, high):
    level, own = 1.0, jax.random.fold_in(key, 6)
    for position, parts in cuts:
        steps = jnp.exp(jax.random.uniform(jax.random.fold_in(own, position), (parts,), jnp.float32, least / len(cuts), high / len(cuts)))
        level = level * jnp.repeat(steps, extent[position] // parts).reshape([-1 if axis == position else 1 for axis in range(len(extent))])
    return level


def normal_values(stream_key, extent, scale, reach, cuts=(), kind=jnp.bfloat16):
    entries = jax.random.normal(stream_key, extent, jnp.float32) * scale
    if len(cuts) > 0:
        entries = level_of(stream_key, extent, cuts, -0.22, 0.18) * entries
    return jnp.clip(entries, min=-reach, max=reach).astype(kind)


def setup_inputs(seed: int = 0) -> dict:
    streams_of = jax.random.split(jax.random.key(seed), 8)
    return {
        "hidden": draw_hidden(jax.random.fold_in(streams_of[7], 71), 0),
        "query_key_value_weight": draw_query_key_value_weight(jax.random.fold_in(streams_of[7], 71), 0),
        "w_out": normal_values(streams_of[2], (QUERY_HEADS * HEAD_SIZE, D), (QUERY_HEADS * HEAD_SIZE) ** -0.5, 0.0625, ((1, 128),)),
        "k_cache": draw_k_cache(jax.random.fold_in(streams_of[7], 71), 0),
        "value_cache": normal_values(streams_of[4], (PROMPT_TOTAL, CONTEXT_SLOTS, KEY_VALUE_HEADS, HEAD_SIZE), 1.0, 6.0, ((0, 16), (2, 8))),
        "lengths": draw_lengths(jax.random.fold_in(streams_of[7], 71), 0),
        "assign": draw_assign(jax.random.fold_in(streams_of[7], 71), 0),
    }


EPS = 1e-06
ROPE_BASE = 1000000.0

def head_norm(vec):
    return vec * lax.rsqrt(lax.optimization_barrier(jnp.mean(vec * vec, axis=-1, keepdims=True)) + EPS)

def rotate(vec, positions):
    half = vec.shape[-1] // 2
    freq = ROPE_BASE ** (-jnp.arange(half, dtype=jnp.float32) * 2.0 / vec.shape[-1])
    angle = positions.astype(jnp.float32)[:, None] * freq[None, :]
    angle = angle.reshape((angle.shape[0],) + (1,) * (vec.ndim - 2) + (half,))
    cosine, sine = (jnp.cos(angle), jnp.sin(angle))
    first, second = (vec[..., :half], vec[..., half:])
    return jnp.concatenate([first * cosine - second * sine, second * cosine + first * sine], axis=-1)

def attend_prompt(inputs):
    query_rows, fresh_key_rows, fresh_value_rows, lens, keys, values = inputs
    scale = HEAD_SIZE ** (-0.5)
    qf = query_rows.astype(jnp.float32)
    scores = jnp.einsum('skjd,ckd->skjc', qf, keys.astype(jnp.float32)) * scale
    own = jnp.einsum('skjd,skd->skj', qf, fresh_key_rows.astype(jnp.float32)) * scale
    mask = (jnp.arange(CONTEXT_SLOTS, dtype=jnp.int32)[None, :] < lens[:, None])[:, None, None, :]
    scores = jnp.where(mask, scores, -jnp.inf)
    top = jnp.maximum(lax.optimization_barrier(jnp.max(scores, axis=-1)), own)
    expo = jnp.where(mask, jnp.exp(scores - top[..., None]), 0.0)
    own_expo = jnp.exp(own - top)
    total = lax.optimization_barrier(jnp.sum(expo, axis=-1)) + own_expo
    weights = (expo / total[..., None]).astype(jnp.bfloat16)
    own_weight = (own_expo / total).astype(jnp.bfloat16)
    mixed = jnp.einsum('skjc,ckd->skjd', weights.astype(jnp.float32), values.astype(jnp.float32))
    mixed = mixed + own_weight.astype(jnp.float32)[..., None] * fresh_value_rows.astype(jnp.float32)[:, :, None, :]
    return mixed.astype(jnp.bfloat16)

def reference(hidden, query_key_value_weight, w_out, k_cache, value_cache, lengths, assign):
    values32 = hidden.astype(jnp.float32)
    normed_rows = (values32 * lax.rsqrt(lax.optimization_barrier(jnp.mean(values32 * values32, axis=-1, keepdims=True)) + EPS)).astype(jnp.bfloat16)
    projected_rows = jnp.dot(normed_rows, query_key_value_weight, preferred_element_type=jnp.float32).reshape(ROW_TOTAL, KEY_VALUE_HEADS, QUERY_PER_KEY + 2, HEAD_SIZE)
    query_rows = rotate(head_norm(projected_rows[:, :, :QUERY_PER_KEY]), lengths).astype(jnp.bfloat16)
    fresh_key_rows = rotate(head_norm(projected_rows[:, :, QUERY_PER_KEY]), lengths).astype(jnp.bfloat16)
    fresh_value_rows = projected_rows[:, :, QUERY_PER_KEY + 1].astype(jnp.bfloat16)
    prompt_id = jnp.arange(ROW_TOTAL, dtype=jnp.int32) // ROWS_GRP * PROMPTS + assign
    sort_order = jnp.argsort(prompt_id, stable=True)
    back = jnp.argsort(sort_order, stable=True)
    ordered_query_rows = query_rows[sort_order].reshape(PROMPT_TOTAL, SAMPLE_COUNT, KEY_VALUE_HEADS, QUERY_PER_KEY, HEAD_SIZE)
    ordered_key_rows = fresh_key_rows[sort_order].reshape(PROMPT_TOTAL, SAMPLE_COUNT, KEY_VALUE_HEADS, HEAD_SIZE)
    ordered_value_rows = fresh_value_rows[sort_order].reshape(PROMPT_TOTAL, SAMPLE_COUNT, KEY_VALUE_HEADS, HEAD_SIZE)
    sorted_lens = lengths[sort_order].reshape(PROMPT_TOTAL, SAMPLE_COUNT)
    mixed = lax.map(attend_prompt, (ordered_query_rows, ordered_key_rows, ordered_value_rows, sorted_lens, k_cache, value_cache))
    mixed = mixed.reshape(ROW_TOTAL, QUERY_HEADS * HEAD_SIZE)[back]
    return jnp.dot(mixed, w_out, preferred_element_type=jnp.float32).astype(jnp.bfloat16)
```

```python
import functools

import jax
import jax.numpy as jnp
import numpy as np
from jax import lax
from jax.experimental import pallas as pl
from jax.experimental.pallas import tpu as pltpu
from jax.sharding import PartitionSpec as P

HEAD_SIZE = 128
PER_KEY = 8
SAMPLES = 8
EPS = 1e-06
ROPE_BASE = 1000000.0
MESH = pl.DeviceIdType.MESH
LOG2E = 1.4426950408889634
MASKED = -1e30
CHUNK = 512

NN = (((1,), (0,)), ((), ()))
NT = (((1,), (1,)), ((), ()))


def dot(a, b, dims=NN):
    return lax.dot_general(a, b, dims, preferred_element_type=jnp.float32)


def layer_kernel(
    size, width, x_ref, w_ref, wo_ref, k_ref, v_ref, len_ref, assign_ref, cos_ref, sin_ref, out_ref,
    xbuf, wbuf, wall, obuf, oall, ssbuf, pbuf, prec, kbuf, vbuf, qs, fresh, lens_sorted, scores, mall, ybuf, yrec,
    local_sem, x_send, x_recv, w_send, w_recv, wf_send, wf_recv, o_send, o_recv, of_send, of_recv,
    ss_send, ss_recv, p_send, p_recv, m_send, m_recv, y_send, y_recv,
):
    g = lax.axis_index("grp")
    t = lax.axis_index("tp")
    q, c = g // 2, g % 2
    rows = x_ref.shape[0]
    head_cols = (PER_KEY + 2) * HEAD_SIZE
    mixed_cols = PER_KEY * HEAD_SIZE
    piece = w_ref.shape[0]
    context = k_ref.shape[1]

    def at(chip, rank):
        return (chip * 2 + c, rank)

    sibling = (q * 2 + 1 - c, t)

    def turn(value, k):
        return lax.rem(value + k, size)

    def remote(src, dst, send, recv, device):
        return pltpu.make_async_remote_copy(
            src_ref=src, dst_ref=dst, send_sem=send, recv_sem=recv, device_id=device, device_id_type=MESH
        )

    k_copy = pltpu.make_async_copy(k_ref, kbuf, local_sem.at[0])
    v_copy = pltpu.make_async_copy(v_ref, vbuf, local_sem.at[1])

    barrier = pltpu.get_barrier_semaphore()

    def greet(device):
        pl.semaphore_signal(barrier, inc=1, device_id=device, device_id_type=MESH)

    greet(sibling)
    for k in range(1, size):
        greet((g, turn(t, k)))
        greet(at(turn(q, k), t))
        greet(at(t, turn(t, k)))
        greet(at(turn(q, k), q))

    @pl.when(q != t)
    def _():
        greet(at(t, t))
        greet(at(q, q))

    pl.semaphore_wait(barrier, jnp.where(q == t, 4 * size - 3, 4 * size - 1))

    def x_copy(k):
        return remote(x_ref, xbuf.at[q], x_send.at[k], x_recv.at[q], at(t, turn(t, k)))

    own_x = pltpu.make_async_copy(x_ref, xbuf.at[q], x_recv.at[q])

    def w_copy(k):
        rank = turn(t, k)
        cols = pl.ds(pl.multiple_of(rank * head_cols, HEAD_SIZE), head_cols)
        return remote(w_ref.at[:, cols], wbuf.at[c, t], w_send.at[k], w_recv.at[t], (g, rank))

    own_cols = pl.ds(pl.multiple_of(t * head_cols, HEAD_SIZE), head_cols)
    own_w = pltpu.make_async_copy(w_ref.at[:, own_cols], wbuf.at[c, t], w_recv.at[t])

    def o_copy(k):
        rank = turn(t, k)
        cols = pl.ds(pl.multiple_of(rank * mixed_cols, HEAD_SIZE), mixed_cols)
        return remote(wo_ref.at[:, cols], obuf.at[c, t], o_send.at[k], o_recv.at[t], (g, rank))

    own_mixed = pl.ds(pl.multiple_of(t * mixed_cols, HEAD_SIZE), mixed_cols)
    own_o = pltpu.make_async_copy(wo_ref.at[:, own_mixed], obuf.at[c, t], o_recv.at[t])

    own_w.start()
    for k in range(1, size):
        w_copy(k).start()

    @pl.when(q == t)
    def _():
        own_x.start()

    @pl.when(q != t)
    def _():
        x_copy(0).start()

    for k in range(1, size):
        x_copy(k).start()
    own_o.start()
    for k in range(1, size):
        o_copy(k).start()
    k_copy.start()
    v_copy.start()

    x32 = x_ref[...].astype(jnp.float32)
    squares = jnp.sum(x32 * x32, axis=-1, keepdims=True)
    lane_row = lax.broadcasted_iota(jnp.int32, (rows, HEAD_SIZE), 0)
    lane_col = lax.broadcasted_iota(jnp.int32, (rows, HEAD_SIZE), 1)
    as_row = jnp.sum(jnp.where(lane_row == lane_col, squares, 0.0), axis=0, keepdims=True)
    ssbuf[t] = jnp.broadcast_to(as_row, (8, HEAD_SIZE))

    def ss_copy(k):
        return remote(ssbuf.at[t], ssbuf.at[t], ss_send.at[k], ss_recv.at[t], (g, turn(t, k)))

    for k in range(1, size):
        ss_copy(k).start()

    assign_row = jnp.broadcast_to(assign_ref[...], (rows, rows))
    i_row = lax.broadcasted_iota(jnp.int32, (rows, rows), 0)
    i_col = lax.broadcasted_iota(jnp.int32, (rows, rows), 1)
    diagonal = i_row == i_col

    def column(row_values):
        return jnp.sum(jnp.where(diagonal, row_values, 0.0), axis=1, keepdims=True)

    assign_f = assign_row.astype(jnp.float32)
    same = assign_f == column(assign_f)
    earlier = jnp.sum(jnp.where(same, jnp.where(i_row < i_col, 1.0, 0.0), 0.0), axis=0, keepdims=True)
    place_row = assign_f * SAMPLES + earlier
    place_col = column(place_row)
    sort_mat = jnp.where(i_row.astype(jnp.float32) == place_row, 1.0, 0.0)
    back_mat = jnp.where(i_col.astype(jnp.float32) == place_col, 1.0, 0.0).astype(jnp.bfloat16)
    len_row = len_ref[...].astype(jnp.float32)
    lens_sorted[...] = jnp.broadcast_to(
        jnp.sum(sort_mat * len_row, axis=1, keepdims=True), (rows, HEAD_SIZE)
    )
    sort_mat = sort_mat.astype(jnp.bfloat16)

    def wf_copy(s):
        return remote(wbuf.at[c, s], wbuf.at[c, s], wf_send.at[s], wf_recv.at[s], sibling)

    def of_copy(s):
        return remote(obuf.at[c, s], obuf.at[c, s], of_send.at[s], of_recv.at[s], sibling)

    def await_into(ref, sem):
        pltpu.make_async_copy(ref, ref, sem).wait()

    for s in range(size):
        await_into(wbuf.at[c, s], w_recv.at[s])
        wf_copy(s).start()
    for s in range(size):
        await_into(wbuf.at[1 - c, s], wf_recv.at[s])
    for core in range(2):
        for s in range(size):
            first = (core * size + s) * piece
            wall[first : first + piece, :] = wbuf[core, s]

    def p_copy(k):
        return remote(pbuf.at[k], prec.at[q], p_send.at[k], p_recv.at[q], at(turn(q, k), t))

    def project(k):
        chip = turn(q, k)
        await_into(xbuf.at[chip], x_recv.at[chip])
        return dot(xbuf[chip], wall[...])

    def project_step(k, carry):
        pbuf[k] = project(k)
        p_copy(k).start()
        return carry

    lax.fori_loop(1, size, project_step, 0)
    prec[q] = project(0)

    for s in range(size):
        await_into(obuf.at[c, s], o_recv.at[s])
        of_copy(s).start()
    for s in range(size):
        await_into(obuf.at[1 - c, s], of_recv.at[s])
    for core in range(2):
        for s in range(size):
            first = (core * size + s) * piece
            oall[first : first + piece, :] = obuf[core, s]

    for k in range(1, size):
        rank = turn(t, k)
        await_into(ssbuf.at[rank], ss_recv.at[rank])
    total_row = ssbuf[0]
    for s in range(1, size):
        total_row = total_row + ssbuf[s]
    total = jnp.sum(jnp.where(lane_row == lane_col, total_row[:1], 0.0), axis=1, keepdims=True)
    row_scale = lax.rsqrt(total * (1.0 / width) + EPS)

    for k in range(1, size):
        chip = turn(q, k)
        await_into(prec.at[chip], p_recv.at[chip])

    cosine, sine = cos_ref[...], sin_ref[...]
    for h in range(PER_KEY + 2):
        cols = slice(h * HEAD_SIZE, (h + 1) * HEAD_SIZE)
        head = prec[0, :, cols]
        for s in range(1, size):
            head = head + prec[s, :, cols]
        head = head * row_scale
        if h <= PER_KEY:
            head = head * lax.rsqrt(jnp.mean(head * head, axis=-1, keepdims=True) + EPS)
            head = head * cosine + pltpu.roll(head, HEAD_SIZE // 2, 1) * sine
        ordered = dot(sort_mat, head.astype(jnp.bfloat16))
        if h < PER_KEY:
            qs[h] = ordered
        else:
            fresh[h - PER_KEY] = ordered

    k_copy.wait()
    v_copy.wait()
    scale2 = HEAD_SIZE ** (-0.5) * LOG2E
    queries = PER_KEY * SAMPLES
    slot_iota = lax.broadcasted_iota(jnp.int32, (queries, HEAD_SIZE), 1).astype(jnp.float32)

    def attend(p):
        mine = pl.ds(pl.multiple_of(p * SAMPLES, SAMPLES), SAMPLES)
        query = qs[:, mine, :]
        own = jnp.sum(query * fresh[0, mine, :][None], axis=-1, keepdims=True).reshape(queries, 1)
        fresh_value = jnp.broadcast_to(fresh[1, mine, :][None], query.shape).reshape(queries, HEAD_SIZE)
        seen = jnp.broadcast_to(lens_sorted[mine, :][None], query.shape).reshape(queries, HEAD_SIZE)
        query = query.reshape(queries, HEAD_SIZE).astype(jnp.bfloat16)
        top = jnp.full((queries, HEAD_SIZE), MASKED, jnp.float32)
        for chunk in range(context // CHUNK):
            part = dot(query, kbuf[p, chunk * CHUNK : (chunk + 1) * CHUNK, :], NT)
            for lane in range(CHUNK // HEAD_SIZE):
                first = chunk * CHUNK + lane * HEAD_SIZE
                tile = part[:, lane * HEAD_SIZE : (lane + 1) * HEAD_SIZE]
                tile = jnp.where(slot_iota < seen - first, tile, MASKED)
                scores[:, first : first + HEAD_SIZE] = tile
                top = jnp.maximum(top, tile)
        peak = jnp.maximum(jnp.max(top, axis=-1, keepdims=True), own)
        shift = peak * scale2
        own_weight = jnp.exp2(own * scale2 - shift)
        sums = jnp.zeros((queries, HEAD_SIZE), jnp.float32)
        mixed = own_weight * fresh_value
        for chunk in range(context // CHUNK):
            cols = slice(chunk * CHUNK, (chunk + 1) * CHUNK)
            weights = jnp.exp2(scores[:, cols] * scale2 - shift)
            for lane in range(CHUNK // HEAD_SIZE):
                sums = sums + weights[:, lane * HEAD_SIZE : (lane + 1) * HEAD_SIZE]
            mixed = mixed + dot(weights.astype(jnp.bfloat16), vbuf[p, cols, :])
        return mixed / (jnp.sum(sums, axis=-1, keepdims=True) + own_weight)

    def m_copy(i, k):
        return remote(mall.at[q, i], mall.at[q, i], m_send.at[i, k], m_recv.at[i, q], at(turn(q, k), t))

    def attend_pair(i, carry):
        low, high = attend(2 * i), attend(2 * i + 1)
        for h in range(PER_KEY):
            part = slice(h * SAMPLES, (h + 1) * SAMPLES)
            mall[q, i, :, h * HEAD_SIZE : (h + 1) * HEAD_SIZE] = jnp.concatenate(
                [low[part], high[part]], axis=0
            ).astype(jnp.bfloat16)
        for k in range(1, size):
            m_copy(i, k).start()
        return carry

    pairs = kbuf.shape[0] // 2
    lax.fori_loop(0, pairs, attend_pair, 0)

    def y_copy(k):
        return remote(ybuf.at[k], yrec.at[t], y_send.at[k], y_recv.at[t], at(turn(q, k), q))

    own_y = pltpu.make_async_copy(ybuf.at[0], yrec.at[t], y_recv.at[t])

    def out_block(k):
        chip = turn(q, k)
        ybuf[k] = dot(mall[chip].reshape(rows, mixed_cols), oall[...], NT)

    out_block(0)

    @pl.when(q == t)
    def _():
        own_y.start()

    @pl.when(q != t)
    def _():
        y_copy(0).start()

    def out_step(k, carry):
        chip = turn(q, k)
        for i in range(pairs):
            await_into(mall.at[chip, i], m_recv.at[i, chip])
        out_block(k)
        y_copy(k).start()
        return carry

    lax.fori_loop(1, size, out_step, 0)

    for s in range(size):
        await_into(yrec.at[s], y_recv.at[s])
    result = yrec[0]
    for s in range(1, size):
        result = result + yrec[s]
    out_ref[...] = dot(back_mat, result.astype(jnp.bfloat16)).astype(jnp.bfloat16)

    @pl.when(q != t)
    def _():
        x_copy(0).wait_send()
        y_copy(0).wait_send()

    for k in range(1, size):
        x_copy(k).wait_send()
        w_copy(k).wait_send()
        o_copy(k).wait_send()
        ss_copy(k).wait_send()
        p_copy(k).wait_send()
        y_copy(k).wait_send()
        for i in range(pairs):
            m_copy(i, k).wait_send()
    for s in range(size):
        wf_copy(s).wait_send()
        of_copy(s).wait_send()


def local(size, hidden, query_key_value_weight, w_out, k_cache, value_cache, lengths, assign):
    rows, features = hidden.shape
    width = features * size
    piece = query_key_value_weight.shape[0]
    prompts, context = k_cache.shape[0], k_cache.shape[1]
    half = HEAD_SIZE // 2
    freq = ROPE_BASE ** (-jnp.arange(half, dtype=jnp.float32) * 2.0 / HEAD_SIZE)
    angle = lengths.astype(jnp.float32)[:, None] * freq[None, :]
    cosine, sine = jnp.cos(angle), jnp.sin(angle)
    cosine = jnp.concatenate([cosine, cosine], axis=1)
    sine = jnp.concatenate([-sine, sine], axis=1)
    head_cols = (PER_KEY + 2) * HEAD_SIZE
    mixed_cols = PER_KEY * HEAD_SIZE
    bf16, f32 = jnp.bfloat16, jnp.float32
    dma = pltpu.SemaphoreType.DMA
    pairs = prompts // 2
    vmem = pl.BlockSpec(memory_space=pltpu.VMEM)
    anywhere = pl.BlockSpec(memory_space=pl.ANY)
    return pl.pallas_call(
        functools.partial(layer_kernel, size, width),
        out_shape=jax.ShapeDtypeStruct((rows, features), bf16),
        in_specs=[vmem, anywhere, anywhere, anywhere, anywhere, vmem, vmem, vmem, vmem],
        out_specs=vmem,
        scratch_shapes=[
            pltpu.VMEM((size, rows, features), bf16),
            pltpu.VMEM((2, size, piece, head_cols), bf16),
            pltpu.VMEM((features, head_cols), bf16),
            pltpu.VMEM((2, size, piece, mixed_cols), bf16),
            pltpu.VMEM((features, mixed_cols), bf16),
            pltpu.VMEM((size, 8, HEAD_SIZE), f32),
            pltpu.VMEM((size, rows, head_cols), f32),
            pltpu.VMEM((size, rows, head_cols), f32),
            pltpu.VMEM((prompts, context, HEAD_SIZE), bf16),
            pltpu.VMEM((prompts, context, HEAD_SIZE), bf16),
            pltpu.VMEM((PER_KEY, rows, HEAD_SIZE), f32),
            pltpu.VMEM((2, rows, HEAD_SIZE), f32),
            pltpu.VMEM((rows, HEAD_SIZE), f32),
            pltpu.VMEM((PER_KEY * SAMPLES, context), f32),
            pltpu.VMEM((size, pairs, 2 * SAMPLES, mixed_cols), bf16),
            pltpu.VMEM((size, rows, features), f32),
            pltpu.VMEM((size, rows, features), f32),
            dma((2,)),
            dma((size,)), dma((size,)),
            dma((size,)), dma((size,)), dma((size,)), dma((size,)),
            dma((size,)), dma((size,)), dma((size,)), dma((size,)),
            dma((size,)), dma((size,)),
            dma((size,)), dma((size,)),
            dma((pairs, size)), dma((pairs, size)),
            dma((size,)), dma((size,)),
        ],
        compiler_params=pltpu.CompilerParams(
            collective_id=0, has_side_effects=True, vmem_limit_bytes=56 * 1024 * 1024
        ),
        name="layer",
    )(
        hidden,
        query_key_value_weight,
        w_out.T,
        k_cache.reshape(prompts, context, HEAD_SIZE),
        value_cache.reshape(prompts, context, HEAD_SIZE),
        lengths.reshape(1, rows),
        assign.reshape(1, rows),
        cosine,
        sine,
    )


def solution(mesh):
    return jax.shard_map(
        functools.partial(local, mesh.shape["tp"]),
        mesh=mesh,
        in_specs=(
            P("grp", "tp"),
            P(("grp", "tp"), None),
            P(None, ("grp", "tp")),
            P("grp", None, "tp", None),
            P("grp", None, "tp", None),
            P("grp"),
            P("grp"),
        ),
        out_specs=P("grp", "tp"),
        check_vma=False,
    )
```

```python
import functools

import jax
import jax.numpy as jnp
import numpy as np
from jax import lax
from jax.experimental import pallas as pl
from jax.experimental.pallas import tpu as pltpu
from jax.sharding import PartitionSpec as P

HEAD_SIZE = 128
PER_KEY = 8
SAMPLES = 8
EPS = 1e-06
ROPE_BASE = 1000000.0
MESH = pl.DeviceIdType.MESH
LOG2E = 1.4426950408889634
MASKED = -1e30
CHUNK = 512
P_TYPE = jnp.bfloat16
Y_TYPE = jnp.bfloat16

NN = (((1,), (0,)), ((), ()))
NT = (((1,), (1,)), ((), ()))


def dot(a, b, dims=NN):
    return lax.dot_general(a, b, dims, preferred_element_type=jnp.float32)


def layer_kernel(
    size, width, x_ref, w_ref, wo_ref, k_ref, v_ref, len_ref, assign_ref, freq_ref, out_ref,
    xgot, xsend, xbuf, wbuf, wall, obuf, oall, pbuf, prec, pown, kbuf, vbuf, qs, fresh, lens_sorted, scores,
    mall, ybuf, yrec, yown, zbuf, zrec,
    local_sem, g_send, g_recv, x_send, x_recv, w_send, w_recv, wf_send, wf_recv, o_send, o_recv, of_send, of_recv,
    p_send, p_recv, m_send, m_recv, y_send, y_recv, z_send, z_recv,
):
    g = lax.axis_index("grp")
    t = lax.axis_index("tp")
    q, c = g // 2, g % 2
    rows = x_ref.shape[0]
    head_cols = (PER_KEY + 2) * HEAD_SIZE
    mixed_cols = PER_KEY * HEAD_SIZE
    piece = w_ref.shape[0]
    context = k_ref.shape[1]
    pairs = k_ref.shape[0] // 2

    sibling = (q * 2 + 1 - c, t)
    mirror = (t * 2 + c, q)

    def turn(value, k):
        return lax.rem(value + k, size)

    def rank_peer(k):
        return (g, turn(t, k))

    def chip_peer(k):
        return (turn(q, k) * 2 + c, t)

    def remote(src, dst, send, recv, device):
        return pltpu.make_async_remote_copy(
            src_ref=src, dst_ref=dst, send_sem=send, recv_sem=recv, device_id=device, device_id_type=MESH
        )

    def await_into(ref, sem):
        pltpu.make_async_copy(ref, ref, sem).wait()

    barrier = pltpu.get_barrier_semaphore()

    def greet(device):
        pl.semaphore_signal(barrier, inc=1, device_id=device, device_id_type=MESH)

    for k in range(1, size):
        greet(rank_peer(k))
        greet(chip_peer(k))
    greet(sibling)

    @pl.when(q != t)
    def _():
        greet(mirror)

    k_copy = pltpu.make_async_copy(k_ref, kbuf, local_sem.at[0])
    v_copy = pltpu.make_async_copy(v_ref, vbuf, local_sem.at[1])
    k_copy.start()
    v_copy.start()

    assign_row = jnp.broadcast_to(assign_ref[...], (rows, rows))
    i_row = lax.broadcasted_iota(jnp.int32, (rows, rows), 0)
    i_col = lax.broadcasted_iota(jnp.int32, (rows, rows), 1)
    diagonal = i_row == i_col

    def column(row_values):
        return jnp.sum(jnp.where(diagonal, row_values, 0.0), axis=1, keepdims=True)

    assign_f = assign_row.astype(jnp.float32)
    same = assign_f == column(assign_f)
    earlier = jnp.sum(jnp.where(same, jnp.where(i_row < i_col, 1.0, 0.0), 0.0), axis=0, keepdims=True)
    place_row = assign_f * SAMPLES + earlier
    place_col = column(place_row)
    sort_mat = jnp.where(i_row.astype(jnp.float32) == place_row, 1.0, 0.0)
    back_mat = jnp.where(i_col.astype(jnp.float32) == place_col, 1.0, 0.0).astype(jnp.bfloat16)
    lens = jnp.sum(sort_mat * len_ref[...].astype(jnp.float32), axis=1, keepdims=True)
    lens_sorted[...] = jnp.broadcast_to(lens, (rows, HEAD_SIZE))
    xgot[t] = dot(sort_mat.astype(jnp.bfloat16), x_ref[...]).astype(jnp.bfloat16)

    pl.semaphore_wait(barrier, jnp.where(q == t, 2 * size - 1, 2 * size))

    def g_copy(k):
        return remote(xgot.at[t], xgot.at[t], g_send.at[k], g_recv.at[t], rank_peer(k))

    def w_copy(k):
        cols = pl.ds(pl.multiple_of(turn(t, k) * head_cols, HEAD_SIZE), head_cols)
        return remote(w_ref.at[:, cols], wbuf.at[c, t], w_send.at[k], w_recv.at[t], rank_peer(k))

    def o_copy(k):
        cols = pl.ds(pl.multiple_of(turn(t, k) * mixed_cols, HEAD_SIZE), mixed_cols)
        return remote(wo_ref.at[:, cols], obuf.at[c, t], o_send.at[k], o_recv.at[t], rank_peer(k))

    own_cols = pl.ds(pl.multiple_of(t * head_cols, HEAD_SIZE), head_cols)
    own_w = pltpu.make_async_copy(w_ref.at[:, own_cols], wbuf.at[c, t], w_recv.at[t])
    own_mixed = pl.ds(pl.multiple_of(t * mixed_cols, HEAD_SIZE), mixed_cols)
    own_o = pltpu.make_async_copy(wo_ref.at[:, own_mixed], obuf.at[c, t], o_recv.at[t])

    for k in range(1, size):
        g_copy(k).start()
    own_w.start()
    own_o.start()
    for k in range(1, size):
        w_copy(k).start()

    angle = lens * freq_ref[...]
    lane = lax.broadcasted_iota(jnp.int32, (rows, HEAD_SIZE), 1)
    cosine = jnp.cos(angle)
    sine = jnp.where(lane < HEAD_SIZE // 2, -1.0, 1.0) * jnp.sin(angle)

    for k in range(1, size):
        await_into(xgot.at[turn(t, k)], g_recv.at[turn(t, k)])
    squares = jnp.zeros((rows, 1), jnp.float32)
    for s in range(size):
        features = xgot[s].astype(jnp.float32)
        squares = squares + jnp.sum(features * features, axis=-1, keepdims=True)
    row_scale = lax.rsqrt(squares * (1.0 / width) + EPS)

    def x_copy(k):
        return remote(xsend.at[turn(q, k)], xbuf.at[q], x_send.at[k], x_recv.at[q], chip_peer(k))

    for k in range(1, size):
        chip = turn(q, k)
        xsend[chip] = (xgot[chip].astype(jnp.float32) * row_scale).astype(jnp.bfloat16)
        x_copy(k).start()
    xsend[q] = (xgot[q].astype(jnp.float32) * row_scale).astype(jnp.bfloat16)

    def wf_copy(s):
        return remote(wbuf.at[c, s], wbuf.at[c, s], wf_send.at[s], wf_recv.at[s], sibling)

    def of_copy(s):
        return remote(obuf.at[c, s], obuf.at[c, s], of_send.at[s], of_recv.at[s], sibling)

    for s in range(size):
        await_into(wbuf.at[c, s], w_recv.at[s])
        wf_copy(s).start()
    for k in range(1, size):
        o_copy(k).start()
    for s in range(size):
        await_into(wbuf.at[1 - c, s], wf_recv.at[s])
    for core in range(2):
        for s in range(size):
            first = (core * size + s) * piece
            wall[first : first + piece, :] = wbuf[core, s]

    def p_copy(k):
        return remote(pbuf.at[k], prec.at[q], p_send.at[k], p_recv.at[q], chip_peer(k))

    def project_step(k, carry):
        chip = turn(q, k)
        await_into(xbuf.at[chip], x_recv.at[chip])
        pbuf[k] = dot(xbuf[chip], wall[...]).astype(pbuf.dtype)
        p_copy(k).start()
        return carry

    lax.fori_loop(1, size, project_step, 0)
    pown[...] = dot(xsend[q], wall[...])

    for s in range(size):
        await_into(obuf.at[c, s], o_recv.at[s])
        of_copy(s).start()
    for s in range(size):
        await_into(obuf.at[1 - c, s], of_recv.at[s])
    for core in range(2):
        for s in range(size):
            first = (core * size + s) * piece
            oall[first : first + piece, :] = obuf[core, s]

    for k in range(1, size):
        await_into(prec.at[turn(q, k)], p_recv.at[turn(q, k)])

    for h in range(PER_KEY + 2):
        cols = slice(h * HEAD_SIZE, (h + 1) * HEAD_SIZE)
        head = pown[:, cols]
        for k in range(1, size):
            head = head + prec[turn(q, k), :, cols].astype(jnp.float32)
        if h <= PER_KEY:
            head = head * lax.rsqrt(jnp.mean(head * head, axis=-1, keepdims=True) + EPS)
            head = head * cosine + pltpu.roll(head, HEAD_SIZE // 2, 1) * sine
        head = head.astype(jnp.bfloat16).astype(jnp.float32)
        if h < PER_KEY:
            qs[h] = head
        else:
            fresh[h - PER_KEY] = head

    k_copy.wait()
    v_copy.wait()
    scale2 = HEAD_SIZE ** (-0.5) * LOG2E
    queries = PER_KEY * SAMPLES
    slot_iota = lax.broadcasted_iota(jnp.int32, (queries, HEAD_SIZE), 1).astype(jnp.float32)

    def attend(p):
        mine = pl.ds(pl.multiple_of(p * SAMPLES, SAMPLES), SAMPLES)
        query = qs[:, mine, :]
        own = jnp.sum(query * fresh[0, mine, :][None], axis=-1, keepdims=True).reshape(queries, 1)
        fresh_value = jnp.broadcast_to(fresh[1, mine, :][None], query.shape).reshape(queries, HEAD_SIZE)
        seen = jnp.broadcast_to(lens_sorted[mine, :][None], query.shape).reshape(queries, HEAD_SIZE)
        query = query.reshape(queries, HEAD_SIZE).astype(jnp.bfloat16)
        top = jnp.full((queries, HEAD_SIZE), MASKED, jnp.float32)
        for chunk in range(context // CHUNK):
            part = dot(query, kbuf[p, chunk * CHUNK : (chunk + 1) * CHUNK, :], NT)
            for lane in range(CHUNK // HEAD_SIZE):
                first = chunk * CHUNK + lane * HEAD_SIZE
                tile = part[:, lane * HEAD_SIZE : (lane + 1) * HEAD_SIZE]
                tile = jnp.where(slot_iota < seen - first, tile, MASKED)
                scores[:, first : first + HEAD_SIZE] = tile
                top = jnp.maximum(top, tile)
        peak = jnp.maximum(jnp.max(top, axis=-1, keepdims=True), own)
        shift = peak * scale2
        own_weight = jnp.exp2(own * scale2 - shift)
        sums = jnp.zeros((queries, HEAD_SIZE), jnp.float32)
        for chunk in range(context // CHUNK):
            cols = slice(chunk * CHUNK, (chunk + 1) * CHUNK)
            weights = jnp.exp2(scores[:, cols] * scale2 - shift)
            scores[:, cols] = weights
            for lane in range(CHUNK // HEAD_SIZE):
                sums = sums + weights[:, lane * HEAD_SIZE : (lane + 1) * HEAD_SIZE]
        part = 1.0 / (jnp.sum(sums, axis=-1, keepdims=True) + own_weight)
        mixed = (own_weight * part).astype(jnp.bfloat16).astype(jnp.float32) * fresh_value
        for chunk in range(context // CHUNK):
            cols = slice(chunk * CHUNK, (chunk + 1) * CHUNK)
            mixed = mixed + dot((scores[:, cols] * part).astype(jnp.bfloat16), vbuf[p, cols, :])
        return mixed

    def m_copy(i, k):
        return remote(mall.at[q, i], mall.at[q, i], m_send.at[i, k], m_recv.at[i, q], chip_peer(k))

    def attend_pair(i, carry):
        low, high = attend(2 * i), attend(2 * i + 1)
        for h in range(PER_KEY):
            part = slice(h * SAMPLES, (h + 1) * SAMPLES)
            mall[q, i, :, h * HEAD_SIZE : (h + 1) * HEAD_SIZE] = jnp.concatenate(
                [low[part], high[part]], axis=0
            ).astype(jnp.bfloat16)
        for k in range(1, size):
            m_copy(i, k).start()
        return carry

    lax.fori_loop(0, pairs, attend_pair, 0)

    def y_copy(k):
        return remote(ybuf.at[k], yrec.at[t], y_send.at[k], y_recv.at[t], rank_peer(k))

    def out_step(k, carry):
        chip = turn(t, k)

        @pl.when(chip != q)
        def _():
            for i in range(pairs):
                await_into(mall.at[chip, i], m_recv.at[i, chip])

        ybuf[k] = dot(mall[chip].reshape(rows, mixed_cols), oall[...], NT).astype(ybuf.dtype)
        y_copy(k).start()
        return carry

    lax.fori_loop(1, size, out_step, 0)

    @pl.when(t != q)
    def _():
        for i in range(pairs):
            await_into(mall.at[t, i], m_recv.at[i, t])

    yown[...] = dot(mall[t].reshape(rows, mixed_cols), oall[...], NT)
    for k in range(1, size):
        await_into(yrec.at[turn(t, k)], y_recv.at[turn(t, k)])
    result = yown[...]
    for k in range(1, size):
        result = result + yrec[turn(t, k)].astype(jnp.float32)
    zbuf[...] = result.astype(jnp.bfloat16)

    z_copy = remote(zbuf, zrec, z_send, z_recv, mirror)

    @pl.when(q != t)
    def _():
        z_copy.start()
        z_copy.wait()

    @pl.when(q == t)
    def _():
        zrec[...] = zbuf[...]

    out_ref[...] = dot(back_mat, zrec[...]).astype(jnp.bfloat16)

    for k in range(1, size):
        g_copy(k).wait_send()
        x_copy(k).wait_send()
        w_copy(k).wait_send()
        o_copy(k).wait_send()
        p_copy(k).wait_send()
        y_copy(k).wait_send()
        for i in range(pairs):
            m_copy(i, k).wait_send()
    for s in range(size):
        wf_copy(s).wait_send()
        of_copy(s).wait_send()


def local(size, hidden, query_key_value_weight, w_out, k_cache, value_cache, lengths, assign):
    rows, features = hidden.shape
    width = features * size
    piece = query_key_value_weight.shape[0]
    prompts, context = k_cache.shape[0], k_cache.shape[1]
    half = np.arange(HEAD_SIZE // 2, dtype=np.float32)
    freq = np.float32(ROPE_BASE) ** (-half * np.float32(2.0) / np.float32(HEAD_SIZE))
    freq = np.concatenate([freq, freq]).astype(np.float32)[None, :]
    head_cols = (PER_KEY + 2) * HEAD_SIZE
    mixed_cols = PER_KEY * HEAD_SIZE
    bf16, f32 = jnp.bfloat16, jnp.float32
    dma = pltpu.SemaphoreType.DMA
    pairs = prompts // 2
    vmem = pl.BlockSpec(memory_space=pltpu.VMEM)
    anywhere = pl.BlockSpec(memory_space=pl.ANY)
    return pl.pallas_call(
        functools.partial(layer_kernel, size, width),
        out_shape=jax.ShapeDtypeStruct((rows, features), bf16),
        in_specs=[vmem, anywhere, anywhere, anywhere, anywhere, vmem, vmem, vmem],
        out_specs=vmem,
        scratch_shapes=[
            pltpu.VMEM((size, rows, features), bf16),
            pltpu.VMEM((size, rows, features), bf16),
            pltpu.VMEM((size, rows, features), bf16),
            pltpu.VMEM((2, size, piece, head_cols), bf16),
            pltpu.VMEM((features, head_cols), bf16),
            pltpu.VMEM((2, size, piece, mixed_cols), bf16),
            pltpu.VMEM((features, mixed_cols), bf16),
            pltpu.VMEM((size, rows, head_cols), P_TYPE),
            pltpu.VMEM((size, rows, head_cols), P_TYPE),
            pltpu.VMEM((rows, head_cols), f32),
            pltpu.VMEM((prompts, context, HEAD_SIZE), bf16),
            pltpu.VMEM((prompts, context, HEAD_SIZE), bf16),
            pltpu.VMEM((PER_KEY, rows, HEAD_SIZE), f32),
            pltpu.VMEM((2, rows, HEAD_SIZE), f32),
            pltpu.VMEM((rows, HEAD_SIZE), f32),
            pltpu.VMEM((PER_KEY * SAMPLES, context), f32),
            pltpu.VMEM((size, pairs, 2 * SAMPLES, mixed_cols), bf16),
            pltpu.VMEM((size, rows, features), Y_TYPE),
            pltpu.VMEM((size, rows, features), Y_TYPE),
            pltpu.VMEM((rows, features), f32),
            pltpu.VMEM((rows, features), bf16),
            pltpu.VMEM((rows, features), bf16),
            dma((2,)),
            dma((size,)), dma((size,)),
            dma((size,)), dma((size,)),
            dma((size,)), dma((size,)), dma((size,)), dma((size,)),
            dma((size,)), dma((size,)), dma((size,)), dma((size,)),
            dma((size,)), dma((size,)),
            dma((pairs, size)), dma((pairs, size)),
            dma((size,)), dma((size,)),
            dma, dma,
        ],
        compiler_params=pltpu.CompilerParams(
            collective_id=0, has_side_effects=True, vmem_limit_bytes=56 * 1024 * 1024
        ),
        name="layer",
    )(
        hidden,
        query_key_value_weight,
        w_out.T,
        k_cache.reshape(prompts, context, HEAD_SIZE),
        value_cache.reshape(prompts, context, HEAD_SIZE),
        lengths.reshape(1, rows),
        assign.reshape(1, rows),
        jnp.asarray(freq),
    )


def solution(mesh):
    return jax.shard_map(
        functools.partial(local, mesh.shape["tp"]),
        mesh=mesh,
        in_specs=(
            P("grp", "tp"),
            P(("grp", "tp"), None),
            P(None, ("grp", "tp")),
            P("grp", None, "tp", None),
            P("grp", None, "tp", None),
            P("grp"),
            P("grp"),
        ),
        out_specs=P("grp", "tp"),
        check_vma=False,
    )
```

```python
import functools

import jax
import jax.numpy as jnp
import numpy as np
from jax import lax
from jax.experimental import pallas as pl
from jax.experimental.pallas import tpu as pltpu
from jax.sharding import PartitionSpec as P

HEAD_SIZE = 128
PER_KEY = 8
SAMPLES = 8
EPS = 1e-06
ROPE_BASE = 1000000.0
MESH = pl.DeviceIdType.MESH
LOG2E = 1.4426950408889634
MASKED = -1e30
CHUNK = 512
P_TYPE = jnp.bfloat16
Y_TYPE = jnp.bfloat16

NN = (((1,), (0,)), ((), ()))
NT = (((1,), (1,)), ((), ()))


def dot(a, b, dims=NN):
    return lax.dot_general(a, b, dims, preferred_element_type=jnp.float32)


def layer_kernel(
    size, width, x_ref, w_ref, wo_ref, k_ref, v_ref, len_ref, assign_ref, freq_ref, out_ref,
    xsort, xgot, xbuf, ranks_sum, rows_scale, wbuf, wall, obuf, oall, pbuf, prec, pown, kbuf, vbuf, qs, fresh, lens_sorted, scores,
    mall, ybuf, yrec, yown, zbuf, zrec,
    local_sem, s_send, s_recv, r_send, r_recv, x_send, x_recv, w_send, w_recv, wf_send, wf_recv, o_send, o_recv, of_send, of_recv,
    p_send, p_recv, m_send, m_recv, y_send, y_recv, z_send, z_recv,
):
    g = lax.axis_index("grp")
    t = lax.axis_index("tp")
    q, c = g // 2, g % 2
    rows = x_ref.shape[0]
    head_cols = (PER_KEY + 2) * HEAD_SIZE
    mixed_cols = PER_KEY * HEAD_SIZE
    piece = w_ref.shape[0]
    context = k_ref.shape[1]
    pairs = k_ref.shape[0] // 2

    sibling = (q * 2 + 1 - c, t)
    mirror = (t * 2 + c, q)

    def turn(value, k):
        return lax.rem(value + k, size)

    def rank_device(rank):
        return (g, rank)

    def chip_device(chip):
        return (chip * 2 + c, t)

    side = size // 2

    def across(value):
        return turn(value, side)

    def along(value, k):
        return value // side * side + lax.rem(lax.rem(value, side) + k, side)

    def remote(src, dst, send, recv, device):
        return pltpu.make_async_remote_copy(
            src_ref=src, dst_ref=dst, send_sem=send, recv_sem=recv, device_id=device, device_id_type=MESH
        )

    def await_into(ref, sem):
        pltpu.make_async_copy(ref, ref, sem).wait()

    barrier = pltpu.get_barrier_semaphore()

    def greet(device):
        pl.semaphore_signal(barrier, inc=1, device_id=device, device_id_type=MESH)

    for k in range(1, size):
        greet(rank_device(turn(t, k)))
        greet(chip_device(turn(q, k)))
        greet((t * 2 + c, turn(t, k)))
        greet((turn(q, k) * 2 + c, q))
    greet(sibling)

    @pl.when(q != t)
    def _():
        greet((t * 2 + c, t))
        greet((q * 2 + c, q))

    k_copy = pltpu.make_async_copy(k_ref, kbuf, local_sem.at[0])
    v_copy = pltpu.make_async_copy(v_ref, vbuf, local_sem.at[1])
    k_copy.start()
    v_copy.start()

    pl.semaphore_wait(barrier, jnp.where(q == t, 4 * size - 3, 4 * size - 1))

    def w_copy(k):
        cols = pl.ds(pl.multiple_of(turn(t, k) * head_cols, HEAD_SIZE), head_cols)
        return remote(w_ref.at[:, cols], wbuf.at[c, t], w_send.at[k], w_recv.at[t], rank_device(turn(t, k)))

    def o_copy(k):
        cols = pl.ds(pl.multiple_of(turn(t, k) * mixed_cols, HEAD_SIZE), mixed_cols)
        return remote(wo_ref.at[:, cols], obuf.at[c, t], o_send.at[k], o_recv.at[t], rank_device(turn(t, k)))

    own_cols = pl.ds(pl.multiple_of(t * head_cols, HEAD_SIZE), head_cols)
    own_w = pltpu.make_async_copy(w_ref.at[:, own_cols], wbuf.at[c, t], w_recv.at[t])
    own_mixed = pl.ds(pl.multiple_of(t * mixed_cols, HEAD_SIZE), mixed_cols)
    own_o = pltpu.make_async_copy(wo_ref.at[:, own_mixed], obuf.at[c, t], o_recv.at[t])

    own_w.start()
    own_o.start()
    for k in range(1, size):
        w_copy(k).start()

    assign_row = jnp.broadcast_to(assign_ref[...], (rows, rows))
    i_row = lax.broadcasted_iota(jnp.int32, (rows, rows), 0)
    i_col = lax.broadcasted_iota(jnp.int32, (rows, rows), 1)
    diagonal = i_row == i_col

    def column(row_values):
        return jnp.sum(jnp.where(diagonal, row_values, 0.0), axis=1, keepdims=True)

    assign_f = assign_row.astype(jnp.float32)
    same = assign_f == column(assign_f)
    earlier = jnp.sum(jnp.where(same, jnp.where(i_row < i_col, 1.0, 0.0), 0.0), axis=0, keepdims=True)
    place_row = assign_f * SAMPLES + earlier
    place_col = column(place_row)
    sort_mat = jnp.where(i_row.astype(jnp.float32) == place_row, 1.0, 0.0)
    back_mat = jnp.where(i_col.astype(jnp.float32) == place_col, 1.0, 0.0).astype(jnp.bfloat16)
    lens = jnp.sum(sort_mat * len_ref[...].astype(jnp.float32), axis=1, keepdims=True)
    lens_sorted[...] = jnp.broadcast_to(lens, (rows, HEAD_SIZE))
    sort_mat = sort_mat.astype(jnp.bfloat16)

    xsort[...] = dot(sort_mat, x_ref[...]).astype(jnp.bfloat16)

    def x_copy(k):
        return remote(xsort, xgot.at[q], x_send.at[k], x_recv.at[q], (t * 2 + c, turn(t, k)))

    own_x = pltpu.make_async_copy(xsort, xgot.at[q], x_recv.at[q])

    @pl.when(q == t)
    def _():
        own_x.start()

    @pl.when(q != t)
    def _():
        x_copy(0).start()

    for k in range(1, size):
        x_copy(k).start()

    lane_diagonal = lax.broadcasted_iota(jnp.int32, (rows, HEAD_SIZE), 0) == lax.broadcasted_iota(
        jnp.int32, (rows, HEAD_SIZE), 1
    )

    def s_copy(k):
        return remote(ranks_sum.at[t], ranks_sum.at[t], s_send.at[k], s_recv.at[t], rank_device(turn(t, k)))

    def r_copy(k):
        return remote(rows_scale.at[q], rows_scale.at[q], r_send.at[k], r_recv.at[q], chip_device(turn(q, k)))

    features = xsort[...].astype(jnp.float32)
    squares = jnp.sum(features * features, axis=-1, keepdims=True)
    ranks_sum[t] = jnp.broadcast_to(
        jnp.sum(jnp.where(lane_diagonal, squares, 0.0), axis=0, keepdims=True), (8, HEAD_SIZE)
    )
    for k in range(1, size):
        s_copy(k).start()

    angle = lens * freq_ref[...]
    lane = lax.broadcasted_iota(jnp.int32, (rows, HEAD_SIZE), 1)
    cosine = jnp.cos(angle)
    sine = jnp.where(lane < HEAD_SIZE // 2, -1.0, 1.0) * jnp.sin(angle)

    for k in range(1, size):
        await_into(ranks_sum.at[turn(t, k)], s_recv.at[turn(t, k)])
    total = ranks_sum[0]
    for s in range(1, size):
        total = total + ranks_sum[s]
    rows_scale[q] = lax.rsqrt(total * (1.0 / width) + EPS)
    for k in range(1, size):
        r_copy(k).start()

    def wf_copy(s):
        return remote(wbuf.at[c, s], wbuf.at[c, s], wf_send.at[s], wf_recv.at[s], sibling)

    def of_copy(s):
        return remote(obuf.at[c, s], obuf.at[c, s], of_send.at[s], of_recv.at[s], sibling)

    for s in range(size):
        await_into(wbuf.at[c, s], w_recv.at[s])
        wf_copy(s).start()
    for s in range(size):
        await_into(wbuf.at[1 - c, s], wf_recv.at[s])
    for core in range(2):
        for s in range(size):
            first = (core * size + s) * piece
            wall[first : first + piece, :] = wbuf[core, s]

    half_rows = rows // 2
    halves = [slice(half * half_rows, (half + 1) * half_rows) for half in range(2)]

    def p_copy(half, chip):
        return remote(
            pbuf.at[half, chip], prec.at[half, q], p_send.at[half, chip], p_recv.at[half, q], chip_device(chip)
        )

    for k in range(1, size):
        await_into(rows_scale.at[turn(q, k)], r_recv.at[turn(q, k)])
    for chip in range(size):
        await_into(xgot.at[chip], x_recv.at[chip])
        scale = jnp.sum(jnp.where(lane_diagonal, rows_scale[chip, :1], 0.0), axis=1, keepdims=True)
        xbuf[chip] = (xgot[chip].astype(jnp.float32) * scale).astype(jnp.bfloat16)

    def project(half):
        def step(k, carry):
            first = lax.rem(q // 2 + k, side) * 2
            block = xbuf[pl.ds(first, 2), halves[half], :].reshape(rows, -1)
            block = dot(block, wall[...])
            for part in range(2):
                chip = first + part

                @pl.when(chip == q)
                def _():
                    pown[half] = block[halves[part]]

                @pl.when(chip != q)
                def _():
                    pbuf[half, chip] = block[halves[part]].astype(pbuf.dtype)
                    p_copy(half, chip).start()

            return carry

        lax.fori_loop(1, side + 1, step, 0)

    project(0)
    project(1)

    def prepare(half):
        for k in range(1, size):
            await_into(prec.at[half, turn(q, k)], p_recv.at[half, turn(q, k)])
        for h in range(PER_KEY + 2):
            cols = slice(h * HEAD_SIZE, (h + 1) * HEAD_SIZE)
            head = pown[half, :, cols]
            for k in range(1, size):
                head = head + prec[half, turn(q, k), :, cols].astype(jnp.float32)
            if h <= PER_KEY:
                head = head * lax.rsqrt(jnp.mean(head * head, axis=-1, keepdims=True) + EPS)
                rolled = pltpu.roll(head, HEAD_SIZE // 2, 1)
                head = head * cosine[halves[half]] + rolled * sine[halves[half]]
            head = head.astype(jnp.bfloat16).astype(jnp.float32)
            if h < PER_KEY:
                qs[h, halves[half], :] = head
            else:
                fresh[h - PER_KEY, halves[half], :] = head

    scale2 = HEAD_SIZE ** (-0.5) * LOG2E
    queries = PER_KEY * SAMPLES
    slot_iota = lax.broadcasted_iota(jnp.int32, (queries, HEAD_SIZE), 1).astype(jnp.float32)

    def attend(p):
        mine = pl.ds(pl.multiple_of(p * SAMPLES, SAMPLES), SAMPLES)
        query = qs[:, mine, :]
        own = jnp.sum(query * fresh[0, mine, :][None], axis=-1, keepdims=True).reshape(queries, 1)
        fresh_value = jnp.broadcast_to(fresh[1, mine, :][None], query.shape).reshape(queries, HEAD_SIZE)
        seen = jnp.broadcast_to(lens_sorted[mine, :][None], query.shape).reshape(queries, HEAD_SIZE)
        query = query.reshape(queries, HEAD_SIZE).astype(jnp.bfloat16)
        top = jnp.full((queries, HEAD_SIZE), MASKED, jnp.float32)
        for chunk in range(context // CHUNK):
            part = dot(query, kbuf[p, chunk * CHUNK : (chunk + 1) * CHUNK, :], NT)
            for lane in range(CHUNK // HEAD_SIZE):
                first = chunk * CHUNK + lane * HEAD_SIZE
                tile = part[:, lane * HEAD_SIZE : (lane + 1) * HEAD_SIZE]
                tile = jnp.where(slot_iota < seen - first, tile, MASKED)
                scores[:, first : first + HEAD_SIZE] = tile
                top = jnp.maximum(top, tile)
        peak = jnp.maximum(jnp.max(top, axis=-1, keepdims=True), own)
        shift = peak * scale2
        own_weight = jnp.exp2(own * scale2 - shift)
        sums = jnp.zeros((queries, HEAD_SIZE), jnp.float32)
        for chunk in range(context // CHUNK):
            cols = slice(chunk * CHUNK, (chunk + 1) * CHUNK)
            weights = jnp.exp2(scores[:, cols] * scale2 - shift)
            scores[:, cols] = weights
            for lane in range(CHUNK // HEAD_SIZE):
                sums = sums + weights[:, lane * HEAD_SIZE : (lane + 1) * HEAD_SIZE]
        part = 1.0 / (jnp.sum(sums, axis=-1, keepdims=True) + own_weight)
        mixed = (own_weight * part).astype(jnp.bfloat16).astype(jnp.float32) * fresh_value
        for chunk in range(context // CHUNK):
            cols = slice(chunk * CHUNK, (chunk + 1) * CHUNK)
            mixed = mixed + dot((scores[:, cols] * part).astype(jnp.bfloat16), vbuf[p, cols, :])
        return mixed

    def m_copy(i, source, chip, sem):
        return remote(
            mall.at[source, i], mall.at[source, i], m_send.at[i, sem], m_recv.at[i, source], chip_device(chip)
        )

    def m_across(i):
        return m_copy(i, q, across(q), 0)

    def m_own(i, k):
        return m_copy(i, q, along(q, k), k)

    def m_passed(i, k):
        return m_copy(i, across(q), along(q, k), side + k)

    def pass_on(i):
        await_into(mall.at[across(q), i], m_recv.at[i, across(q)])
        for k in range(1, side):
            m_passed(i, k).start()

    def attend_pair(i, carry):
        low, high = attend(2 * i), attend(2 * i + 1)
        for h in range(PER_KEY):
            part = slice(h * SAMPLES, (h + 1) * SAMPLES)
            mall[q, i, :, h * HEAD_SIZE : (h + 1) * HEAD_SIZE] = jnp.concatenate(
                [low[part], high[part]], axis=0
            ).astype(jnp.bfloat16)
        m_across(i).start()
        for k in range(1, side):
            m_own(i, k).start()

        @pl.when(i > 0)
        def _():
            pass_on(i - 1)

        return carry

    prepare(0)
    for k in range(1, size):
        o_copy(k).start()
    k_copy.wait()
    v_copy.wait()
    lax.fori_loop(0, pairs // 2, attend_pair, 0)
    prepare(1)
    lax.fori_loop(pairs // 2, pairs - 1, attend_pair, 0)
    for s in range(size):
        await_into(obuf.at[c, s], o_recv.at[s])
        of_copy(s).start()
    attend_pair(pairs - 1, 0)
    pass_on(pairs - 1)
    for s in range(size):
        await_into(obuf.at[1 - c, s], of_recv.at[s])
    for core in range(2):
        for s in range(size):
            first = (core * size + s) * piece
            oall[first : first + piece, :] = obuf[core, s]

    def y_copy(half, rank):
        return remote(
            ybuf.at[half, rank], yrec.at[half, t], y_send.at[half, rank], y_recv.at[half, t], rank_device(rank)
        )

    half_pairs = pairs // 2

    def project_out(half):
        def step(k, carry):
            first = lax.rem(t // 2 + k, side) * 2
            for part in range(2):
                chip = first + part

                @pl.when((chip != q) & (chip != across(q)))
                def _():
                    for i in range(half * half_pairs, (half + 1) * half_pairs):
                        await_into(mall.at[chip, i], m_recv.at[i, chip])

            block = mall[pl.ds(first, 2), half * half_pairs : (half + 1) * half_pairs]
            block = dot(block.reshape(rows, mixed_cols), oall[...], NT)
            for part in range(2):
                rank = first + part

                @pl.when(rank == t)
                def _():
                    yown[half] = block[halves[part]]

                @pl.when(rank != t)
                def _():
                    ybuf[half, rank] = block[halves[part]].astype(ybuf.dtype)
                    y_copy(half, rank).start()

            return carry

        lax.fori_loop(1, side + 1, step, 0)

    def z_copy(half):
        return remote(zbuf.at[half], zrec.at[half], z_send.at[half], z_recv.at[half], mirror)

    project_out(0)
    project_out(1)
    for half in range(2):
        result = yown[half]
        for k in range(1, size):
            await_into(yrec.at[half, turn(t, k)], y_recv.at[half, turn(t, k)])
        for k in range(1, size):
            result = result + yrec[half, turn(t, k)].astype(jnp.float32)
        zbuf[half] = result.astype(jnp.bfloat16)

        @pl.when(q != t)
        def _():
            z_copy(half).start()

    @pl.when(q != t)
    def _():
        for half in range(2):
            z_copy(half).wait()

    @pl.when(q == t)
    def _():
        zrec[...] = zbuf[...]

    out_ref[...] = dot(back_mat, zrec[...].reshape(rows, -1)).astype(jnp.bfloat16)

    @pl.when(q != t)
    def _():
        x_copy(0).wait_send()

    for k in range(1, size):
        x_copy(k).wait_send()
        s_copy(k).wait_send()
        r_copy(k).wait_send()
        w_copy(k).wait_send()
        o_copy(k).wait_send()
        for half in range(2):
            p_copy(half, turn(q, k)).wait_send()
            y_copy(half, turn(t, k)).wait_send()
    for i in range(pairs):
        m_across(i).wait_send()
        for k in range(1, side):
            m_own(i, k).wait_send()
            m_passed(i, k).wait_send()
    for s in range(size):
        wf_copy(s).wait_send()
        of_copy(s).wait_send()


def local(size, hidden, query_key_value_weight, w_out, k_cache, value_cache, lengths, assign):
    rows, features = hidden.shape
    width = features * size
    piece = query_key_value_weight.shape[0]
    prompts, context = k_cache.shape[0], k_cache.shape[1]
    half = np.arange(HEAD_SIZE // 2, dtype=np.float32)
    freq = np.float32(ROPE_BASE) ** (-half * np.float32(2.0) / np.float32(HEAD_SIZE))
    freq = np.concatenate([freq, freq]).astype(np.float32)[None, :]
    head_cols = (PER_KEY + 2) * HEAD_SIZE
    mixed_cols = PER_KEY * HEAD_SIZE
    bf16, f32 = jnp.bfloat16, jnp.float32
    dma = pltpu.SemaphoreType.DMA
    pairs = prompts // 2
    vmem = pl.BlockSpec(memory_space=pltpu.VMEM)
    anywhere = pl.BlockSpec(memory_space=pl.ANY)
    return pl.pallas_call(
        functools.partial(layer_kernel, size, width),
        out_shape=jax.ShapeDtypeStruct((rows, features), bf16),
        in_specs=[vmem, anywhere, anywhere, anywhere, anywhere, vmem, vmem, vmem],
        out_specs=vmem,
        scratch_shapes=[
            pltpu.VMEM((rows, features), bf16),
            pltpu.VMEM((size, rows, features), bf16),
            pltpu.VMEM((size, rows, features), bf16),
            pltpu.VMEM((size, 8, HEAD_SIZE), f32),
            pltpu.VMEM((size, 8, HEAD_SIZE), f32),
            pltpu.VMEM((2, size, piece, head_cols), bf16),
            pltpu.VMEM((features, head_cols), bf16),
            pltpu.VMEM((2, size, piece, mixed_cols), bf16),
            pltpu.VMEM((features, mixed_cols), bf16),
            pltpu.VMEM((2, size, rows // 2, head_cols), P_TYPE),
            pltpu.VMEM((2, size, rows // 2, head_cols), P_TYPE),
            pltpu.VMEM((2, rows // 2, head_cols), f32),
            pltpu.VMEM((prompts, context, HEAD_SIZE), bf16),
            pltpu.VMEM((prompts, context, HEAD_SIZE), bf16),
            pltpu.VMEM((PER_KEY, rows, HEAD_SIZE), f32),
            pltpu.VMEM((2, rows, HEAD_SIZE), f32),
            pltpu.VMEM((rows, HEAD_SIZE), f32),
            pltpu.VMEM((PER_KEY * SAMPLES, context), f32),
            pltpu.VMEM((size, pairs, 2 * SAMPLES, mixed_cols), bf16),
            pltpu.VMEM((2, size, rows // 2, features), Y_TYPE),
            pltpu.VMEM((2, size, rows // 2, features), Y_TYPE),
            pltpu.VMEM((2, rows // 2, features), f32),
            pltpu.VMEM((2, rows // 2, features), bf16),
            pltpu.VMEM((2, rows // 2, features), bf16),
            dma((2,)),
            dma((size,)), dma((size,)), dma((size,)), dma((size,)),
            dma((size,)), dma((size,)),
            dma((size,)), dma((size,)), dma((size,)), dma((size,)),
            dma((size,)), dma((size,)), dma((size,)), dma((size,)),
            dma((2, size)), dma((2, size)),
            dma((pairs, size)), dma((pairs, size)),
            dma((2, size)), dma((2, size)),
            dma((2,)), dma((2,)),
        ],
        compiler_params=pltpu.CompilerParams(
            collective_id=0, has_side_effects=True, vmem_limit_bytes=56 * 1024 * 1024
        ),
        name="layer",
    )(
        hidden,
        query_key_value_weight,
        w_out.T,
        k_cache.reshape(prompts, context, HEAD_SIZE),
        value_cache.reshape(prompts, context, HEAD_SIZE),
        lengths.reshape(1, rows),
        assign.reshape(1, rows),
        jnp.asarray(freq),
    )


def solution(mesh):
    return jax.shard_map(
        functools.partial(local, mesh.shape["tp"]),
        mesh=mesh,
        in_specs=(
            P("grp", "tp"),
            P(("grp", "tp"), None),
            P(None, ("grp", "tp")),
            P("grp", None, "tp", None),
            P("grp", None, "tp", None),
            P("grp"),
            P("grp"),
        ),
        out_specs=P("grp", "tp"),
        check_vma=False,
    )
```

```python
import functools

import jax
import jax.numpy as jnp
import numpy as np
from jax import lax
from jax.experimental import pallas as pl
from jax.experimental.pallas import tpu as pltpu
from jax.sharding import PartitionSpec as P

HEAD_SIZE = 128
PER_KEY = 8
SAMPLES = 8
EPS = 1e-06
ROPE_BASE = 1000000.0
MESH = pl.DeviceIdType.MESH
LOG2E = 1.4426950408889634
MASKED = -1e30
CHUNK = 512
P_TYPE = jnp.bfloat16
Y_TYPE = jnp.bfloat16

NN = (((1,), (0,)), ((), ()))
NT = (((1,), (1,)), ((), ()))


def dot(a, b, dims=NN):
    return lax.dot_general(a, b, dims, preferred_element_type=jnp.float32)


def layer_kernel(
    size, width, x_ref, w_ref, wo_ref, k_ref, v_ref, len_ref, assign_ref, freq_ref, out_ref,
    xsort, xgot, xbuf, ranks_sum, rows_scale, wbuf, wall, obuf, oall, pbuf, prec, pown, kbuf, vbuf, qs, fresh, lens_sorted, scores,
    mall, ybuf, yrec, yown, zbuf, zrec,
    local_sem, s_send, s_recv, r_send, r_recv, x_send, x_recv, w_send, w_recv, wf_send, wf_recv, o_send, o_recv, of_send, of_recv,
    p_send, p_recv, m_send, m_recv, y_send, y_recv, z_send, z_recv,
):
    g = lax.axis_index("grp")
    t = lax.axis_index("tp")
    q, c = g // 2, g % 2
    rows = x_ref.shape[0]
    head_cols = (PER_KEY + 2) * HEAD_SIZE
    mixed_cols = PER_KEY * HEAD_SIZE
    piece = w_ref.shape[0]
    context = k_ref.shape[1]
    pairs = k_ref.shape[0] // 2

    sibling = (q * 2 + 1 - c, t)

    def summing_rank(chip):
        return chip % (size // 2) * 2 + chip // (size // 2)

    summed_chip = t % 2 * (size // 2) + t // 2
    alone = (summed_chip == q) & (q == t)

    def turn(value, k):
        return lax.rem(value + k, size)

    def rank_device(rank):
        return (g, rank)

    def chip_device(chip):
        return (chip * 2 + c, t)

    side = size // 2

    def across(value):
        return turn(value, side)

    def along(value, k):
        return value // side * side + lax.rem(lax.rem(value, side) + k, side)

    def remote(src, dst, send, recv, device):
        return pltpu.make_async_remote_copy(
            src_ref=src, dst_ref=dst, send_sem=send, recv_sem=recv, device_id=device, device_id_type=MESH
        )

    def await_into(ref, sem):
        pltpu.make_async_copy(ref, ref, sem).wait()

    barrier = pltpu.get_barrier_semaphore()

    def greet(device):
        pl.semaphore_signal(barrier, inc=1, device_id=device, device_id_type=MESH)

    for k in range(1, size):
        greet(rank_device(turn(t, k)))
        greet(chip_device(turn(q, k)))
        greet((t * 2 + c, turn(t, k)))
        greet((turn(q, k) * 2 + c, q))
    greet(sibling)

    @pl.when(q != t)
    def _():
        greet((t * 2 + c, t))
        greet((q * 2 + c, q))

    k_copy = pltpu.make_async_copy(k_ref, kbuf, local_sem.at[0])
    v_copy = pltpu.make_async_copy(v_ref, vbuf, local_sem.at[1])
    k_copy.start()
    v_copy.start()

    assign_row = jnp.broadcast_to(assign_ref[...], (rows, rows))
    i_row = lax.broadcasted_iota(jnp.int32, (rows, rows), 0)
    i_col = lax.broadcasted_iota(jnp.int32, (rows, rows), 1)
    diagonal = i_row == i_col

    def column(row_values):
        return jnp.sum(jnp.where(diagonal, row_values, 0.0), axis=1, keepdims=True)

    assign_f = assign_row.astype(jnp.float32)
    same = assign_f == column(assign_f)
    earlier = jnp.sum(jnp.where(same, jnp.where(i_row < i_col, 1.0, 0.0), 0.0), axis=0, keepdims=True)
    place_row = assign_f * SAMPLES + earlier
    place_col = column(place_row)
    sort_mat = jnp.where(i_row.astype(jnp.float32) == place_row, 1.0, 0.0)
    back_mat = jnp.where(i_col.astype(jnp.float32) == place_col, 1.0, 0.0).astype(jnp.bfloat16)
    lens = jnp.sum(sort_mat * len_ref[...].astype(jnp.float32), axis=1, keepdims=True)
    lens_sorted[...] = jnp.broadcast_to(lens, (rows, HEAD_SIZE))
    sort_mat = sort_mat.astype(jnp.bfloat16)

    xsort[...] = dot(sort_mat, x_ref[...]).astype(jnp.bfloat16)

    lane_diagonal = lax.broadcasted_iota(jnp.int32, (rows, HEAD_SIZE), 0) == lax.broadcasted_iota(
        jnp.int32, (rows, HEAD_SIZE), 1
    )

    features = xsort[...].astype(jnp.float32)
    squares = jnp.sum(features * features, axis=-1, keepdims=True)
    ranks_sum[t] = jnp.broadcast_to(
        jnp.sum(jnp.where(lane_diagonal, squares, 0.0), axis=0, keepdims=True), (8, HEAD_SIZE)
    )

    pl.semaphore_wait(barrier, jnp.where(q == t, 4 * size - 3, 4 * size - 1))

    part_cols = head_cols // 2

    def w_cols(part, rank):
        return pl.ds(pl.multiple_of(rank * head_cols + part * part_cols, HEAD_SIZE), part_cols)

    def w_copy(part, k):
        rank = turn(t, k)
        return remote(
            w_ref.at[:, w_cols(part, rank)], wbuf.at[part, c, t], w_send.at[part, k], w_recv.at[part, t], rank_device(rank)
        )

    def o_copy(k):
        cols = pl.ds(pl.multiple_of(turn(t, k) * mixed_cols, HEAD_SIZE), mixed_cols)
        return remote(wo_ref.at[:, cols], obuf.at[c, t], o_send.at[k], o_recv.at[t], rank_device(turn(t, k)))

    def own_w(part):
        return pltpu.make_async_copy(w_ref.at[:, w_cols(part, t)], wbuf.at[part, c, t], w_recv.at[part, t])

    own_mixed = pl.ds(pl.multiple_of(t * mixed_cols, HEAD_SIZE), mixed_cols)
    own_o = pltpu.make_async_copy(wo_ref.at[:, own_mixed], obuf.at[c, t], o_recv.at[t])

    def x_copy(k):
        return remote(xsort, xgot.at[q], x_send.at[k], x_recv.at[q], (t * 2 + c, turn(t, k)))

    own_x = pltpu.make_async_copy(xsort, xgot.at[q], x_recv.at[q])

    @pl.when(q == t)
    def _():
        own_x.start()

    @pl.when(q != t)
    def _():
        x_copy(0).start()

    for k in range(1, size):
        x_copy(k).start()

    def s_copy(k):
        return remote(ranks_sum.at[t], ranks_sum.at[t], s_send.at[k], s_recv.at[t], rank_device(turn(t, k)))

    def r_copy(k):
        return remote(rows_scale.at[q], rows_scale.at[q], r_send.at[k], r_recv.at[q], chip_device(turn(q, k)))

    for k in range(1, size):
        s_copy(k).start()

    for part in range(2):
        own_w(part).start()
        for k in range(1, size):
            w_copy(part, k).start()
    own_o.start()

    angle = lens * freq_ref[...]
    lane = lax.broadcasted_iota(jnp.int32, (rows, HEAD_SIZE), 1)
    cosine = jnp.cos(angle)
    sine = jnp.where(lane < HEAD_SIZE // 2, -1.0, 1.0) * jnp.sin(angle)

    for k in range(1, size):
        await_into(ranks_sum.at[turn(t, k)], s_recv.at[turn(t, k)])
    total = ranks_sum[0]
    for s in range(1, size):
        total = total + ranks_sum[s]
    rows_scale[q] = lax.rsqrt(total * (1.0 / width) + EPS)
    for k in range(1, size):
        r_copy(k).start()

    def wf_copy(part, s):
        piece_at = wbuf.at[part, c, s]
        return remote(piece_at, piece_at, wf_send.at[part, s], wf_recv.at[part, s], sibling)

    def of_copy(s):
        return remote(obuf.at[c, s], obuf.at[c, s], of_send.at[s], of_recv.at[s], sibling)

    def gather_weights(part):
        for k in range(size):
            s = turn(t, size - k)
            await_into(wbuf.at[part, c, s], w_recv.at[part, s])
            wf_copy(part, s).start()
        for s in range(size):
            await_into(wbuf.at[part, 1 - c, s], wf_recv.at[part, s])
        for core in range(2):
            for s in range(size):
                first = (core * size + s) * piece
                wall[part, first : first + piece, :] = wbuf[part, core, s]

    gather_weights(0)

    half_rows = rows // 2
    halves = [slice(half * half_rows, (half + 1) * half_rows) for half in range(2)]

    def p_copy(part, half, chip):
        return remote(
            pbuf.at[part, half, chip],
            prec.at[part, half, q],
            p_send.at[part, half, chip],
            p_recv.at[part, half, q],
            chip_device(chip),
        )

    for k in range(1, size):
        await_into(rows_scale.at[turn(q, k)], r_recv.at[turn(q, k)])
    for chip in range(size):
        await_into(xgot.at[chip], x_recv.at[chip])
        scale = jnp.sum(jnp.where(lane_diagonal, rows_scale[chip, :1], 0.0), axis=1, keepdims=True)
        xbuf[chip] = (xgot[chip].astype(jnp.float32) * scale).astype(jnp.bfloat16)

    def project(part, half):
        block = dot(xbuf[:, halves[half], :].reshape(size * half_rows, -1), wall[part])
        for chip in range(size):
            result = block[chip * half_rows : (chip + 1) * half_rows]

            @pl.when(chip == q)
            def _():
                pown[part, half] = result

            @pl.when(chip != q)
            def _():
                pbuf[part, half, chip] = result.astype(pbuf.dtype)
                p_copy(part, half, chip).start()

    project(0, 0)
    gather_weights(1)
    project(1, 0)
    project(0, 1)
    project(1, 1)

    def prepare(half):
        for k in range(1, size):
            for part in range(2):
                await_into(prec.at[part, half, turn(q, k)], p_recv.at[part, half, turn(q, k)])
        for h in range(PER_KEY + 2):
            part, place = divmod(h, (PER_KEY + 2) // 2)
            cols = slice(place * HEAD_SIZE, (place + 1) * HEAD_SIZE)
            head = pown[part, half, :, cols]
            for k in range(1, size):
                head = head + prec[part, half, turn(q, k), :, cols].astype(jnp.float32)
            if h <= PER_KEY:
                head = head * lax.rsqrt(jnp.mean(head * head, axis=-1, keepdims=True) + EPS)
                rolled = pltpu.roll(head, HEAD_SIZE // 2, 1)
                head = head * cosine[halves[half]] + rolled * sine[halves[half]]
            head = head.astype(jnp.bfloat16).astype(jnp.float32)
            if h < PER_KEY:
                qs[h, halves[half], :] = head
            else:
                fresh[h - PER_KEY, halves[half], :] = head

    scale2 = HEAD_SIZE ** (-0.5) * LOG2E
    queries = PER_KEY * SAMPLES
    slot_iota = lax.broadcasted_iota(jnp.int32, (queries, HEAD_SIZE), 1).astype(jnp.float32)

    def attend(p):
        mine = pl.ds(pl.multiple_of(p * SAMPLES, SAMPLES), SAMPLES)
        query = qs[:, mine, :]
        own = jnp.sum(query * fresh[0, mine, :][None], axis=-1, keepdims=True).reshape(queries, 1)
        fresh_value = jnp.broadcast_to(fresh[1, mine, :][None], query.shape).reshape(queries, HEAD_SIZE)
        seen = jnp.broadcast_to(lens_sorted[mine, :][None], query.shape).reshape(queries, HEAD_SIZE)
        query = query.reshape(queries, HEAD_SIZE).astype(jnp.bfloat16)
        top = jnp.full((queries, HEAD_SIZE), MASKED, jnp.float32)
        for chunk in range(context // CHUNK):
            part = dot(query, kbuf[p, chunk * CHUNK : (chunk + 1) * CHUNK, :], NT)
            for lane in range(CHUNK // HEAD_SIZE):
                first = chunk * CHUNK + lane * HEAD_SIZE
                tile = part[:, lane * HEAD_SIZE : (lane + 1) * HEAD_SIZE]
                tile = jnp.where(slot_iota < seen - first, tile, MASKED)
                scores[:, first : first + HEAD_SIZE] = tile
                top = jnp.maximum(top, tile)
        peak = jnp.maximum(jnp.max(top, axis=-1, keepdims=True), own)
        shift = peak * scale2
        own_weight = jnp.exp2(own * scale2 - shift)
        sums = jnp.zeros((queries, HEAD_SIZE), jnp.float32)
        for chunk in range(context // CHUNK):
            cols = slice(chunk * CHUNK, (chunk + 1) * CHUNK)
            weights = jnp.exp2(scores[:, cols] * scale2 - shift)
            scores[:, cols] = weights
            for lane in range(CHUNK // HEAD_SIZE):
                sums = sums + weights[:, lane * HEAD_SIZE : (lane + 1) * HEAD_SIZE]
        part = 1.0 / (jnp.sum(sums, axis=-1, keepdims=True) + own_weight)
        mixed = (own_weight * part).astype(jnp.bfloat16).astype(jnp.float32) * fresh_value
        for chunk in range(context // CHUNK):
            cols = slice(chunk * CHUNK, (chunk + 1) * CHUNK)
            mixed = mixed + dot((scores[:, cols] * part).astype(jnp.bfloat16), vbuf[p, cols, :])
        return mixed

    def m_copy(i, source, chip, sem):
        return remote(
            mall.at[source, i], mall.at[source, i], m_send.at[i, sem], m_recv.at[i, source], chip_device(chip)
        )

    def m_across(i):
        return m_copy(i, q, across(q), 0)

    def m_own(i, k):
        return m_copy(i, q, along(q, k), k)

    def m_passed(i, k):
        return m_copy(i, across(q), along(q, k), side + k)

    def pass_on(i):
        await_into(mall.at[across(q), i], m_recv.at[i, across(q)])
        for k in range(1, side):
            m_passed(i, k).start()

    def attend_pair(i):
        low, high = attend(2 * i), attend(2 * i + 1)
        for h in range(PER_KEY):
            part = slice(h * SAMPLES, (h + 1) * SAMPLES)
            mall[q, i, :, h * HEAD_SIZE : (h + 1) * HEAD_SIZE] = jnp.concatenate(
                [low[part], high[part]], axis=0
            ).astype(jnp.bfloat16)

    prepare(0)
    k_copy.wait()
    v_copy.wait()
    for i in range(pairs):
        if i == 1:
            for k in range(1, size):
                o_copy(k).start()
        if i == pairs // 2:
            prepare(1)
        if i == pairs - 1:
            for s in range(size):
                await_into(obuf.at[c, s], o_recv.at[s])
                of_copy(s).start()
        attend_pair(i)
        m_across(i).start()
        for k in range(1, side):
            m_own(i, k).start()
        if i > 0:
            pass_on(i - 1)
    pass_on(pairs - 1)
    for s in range(size):
        await_into(obuf.at[1 - c, s], of_recv.at[s])
    for core in range(2):
        for s in range(size):
            first = (core * size + s) * piece
            oall[first : first + piece, :] = obuf[core, s]

    def y_copy(half, rank):
        return remote(
            ybuf.at[half, rank], yrec.at[half, t], y_send.at[half, rank], y_recv.at[half, t], rank_device(rank)
        )

    half_pairs = pairs // 2

    def project_out(half):
        for chip in range(size):
            for i in range(half * half_pairs, (half + 1) * half_pairs):

                @pl.when((chip != q) & (chip != across(q)))
                def _():
                    await_into(mall.at[chip, i], m_recv.at[i, chip])

        block = mall[:, half * half_pairs : (half + 1) * half_pairs].reshape(size * half_rows, mixed_cols)
        block = dot(block, oall[...], NT)
        for chip in range(size):
            rank = summing_rank(chip)
            result = block[chip * half_rows : (chip + 1) * half_rows]

            @pl.when(rank == t)
            def _():
                yown[half] = result

            @pl.when(rank != t)
            def _():
                ybuf[half, rank] = result.astype(ybuf.dtype)
                y_copy(half, rank).start()

    def z_copy(half):
        return remote(zbuf.at[half], zrec.at[half], z_send.at[half], z_recv.at[half], (summed_chip * 2 + c, q))

    project_out(0)
    project_out(1)
    for half in range(2):
        result = yown[half]
        for k in range(1, size):
            await_into(yrec.at[half, turn(t, k)], y_recv.at[half, turn(t, k)])
        for k in range(1, size):
            result = result + yrec[half, turn(t, k)].astype(jnp.float32)
        zbuf[half] = result.astype(jnp.bfloat16)

        @pl.when(jnp.logical_not(alone))
        def _():
            z_copy(half).start()

    @pl.when(jnp.logical_not(alone))
    def _():
        for half in range(2):
            z_copy(half).wait()

    @pl.when(alone)
    def _():
        zrec[...] = zbuf[...]

    out_ref[...] = dot(back_mat, zrec[...].reshape(rows, -1)).astype(jnp.bfloat16)

    @pl.when(q != t)
    def _():
        x_copy(0).wait_send()

    for k in range(1, size):
        x_copy(k).wait_send()
        s_copy(k).wait_send()
        r_copy(k).wait_send()
        for part in range(2):
            w_copy(part, k).wait_send()
        o_copy(k).wait_send()
        for half in range(2):
            for part in range(2):
                p_copy(part, half, turn(q, k)).wait_send()
            y_copy(half, turn(t, k)).wait_send()
    for i in range(pairs):
        m_across(i).wait_send()
        for k in range(1, side):
            m_own(i, k).wait_send()
            m_passed(i, k).wait_send()
    for s in range(size):
        for part in range(2):
            wf_copy(part, s).wait_send()
        of_copy(s).wait_send()


def local(size, hidden, query_key_value_weight, w_out, k_cache, value_cache, lengths, assign):
    rows, features = hidden.shape
    width = features * size
    piece = query_key_value_weight.shape[0]
    prompts, context = k_cache.shape[0], k_cache.shape[1]
    half = np.arange(HEAD_SIZE // 2, dtype=np.float32)
    freq = np.float32(ROPE_BASE) ** (-half * np.float32(2.0) / np.float32(HEAD_SIZE))
    freq = np.concatenate([freq, freq]).astype(np.float32)[None, :]
    head_cols = (PER_KEY + 2) * HEAD_SIZE
    mixed_cols = PER_KEY * HEAD_SIZE
    bf16, f32 = jnp.bfloat16, jnp.float32
    dma = pltpu.SemaphoreType.DMA
    pairs = prompts // 2
    vmem = pl.BlockSpec(memory_space=pltpu.VMEM)
    anywhere = pl.BlockSpec(memory_space=pl.ANY)
    return pl.pallas_call(
        functools.partial(layer_kernel, size, width),
        out_shape=jax.ShapeDtypeStruct((rows, features), bf16),
        in_specs=[vmem, anywhere, anywhere, anywhere, anywhere, vmem, vmem, vmem],
        out_specs=vmem,
        scratch_shapes=[
            pltpu.VMEM((rows, features), bf16),
            pltpu.VMEM((size, rows, features), bf16),
            pltpu.VMEM((size, rows, features), bf16),
            pltpu.VMEM((size, 8, HEAD_SIZE), f32),
            pltpu.VMEM((size, 8, HEAD_SIZE), f32),
            pltpu.VMEM((2, 2, size, piece, head_cols // 2), bf16),
            pltpu.VMEM((2, features, head_cols // 2), bf16),
            pltpu.VMEM((2, size, piece, mixed_cols), bf16),
            pltpu.VMEM((features, mixed_cols), bf16),
            pltpu.VMEM((2, 2, size, rows // 2, head_cols // 2), P_TYPE),
            pltpu.VMEM((2, 2, size, rows // 2, head_cols // 2), P_TYPE),
            pltpu.VMEM((2, 2, rows // 2, head_cols // 2), f32),
            pltpu.VMEM((prompts, context, HEAD_SIZE), bf16),
            pltpu.VMEM((prompts, context, HEAD_SIZE), bf16),
            pltpu.VMEM((PER_KEY, rows, HEAD_SIZE), f32),
            pltpu.VMEM((2, rows, HEAD_SIZE), f32),
            pltpu.VMEM((rows, HEAD_SIZE), f32),
            pltpu.VMEM((PER_KEY * SAMPLES, context), f32),
            pltpu.VMEM((size, pairs, 2 * SAMPLES, mixed_cols), bf16),
            pltpu.VMEM((2, size, rows // 2, features), Y_TYPE),
            pltpu.VMEM((2, size, rows // 2, features), Y_TYPE),
            pltpu.VMEM((2, rows // 2, features), f32),
            pltpu.VMEM((2, rows // 2, features), bf16),
            pltpu.VMEM((2, rows // 2, features), bf16),
            dma((2,)),
            dma((size,)), dma((size,)), dma((size,)), dma((size,)),
            dma((size,)), dma((size,)),
            dma((2, size)), dma((2, size)), dma((2, size)), dma((2, size)),
            dma((size,)), dma((size,)), dma((size,)), dma((size,)),
            dma((2, 2, size)), dma((2, 2, size)),
            dma((pairs, size)), dma((pairs, size)),
            dma((2, size)), dma((2, size)),
            dma((2,)), dma((2,)),
        ],
        compiler_params=pltpu.CompilerParams(
            collective_id=0, has_side_effects=True, vmem_limit_bytes=56 * 1024 * 1024
        ),
        name="layer",
    )(
        hidden,
        query_key_value_weight,
        w_out.T,
        k_cache.reshape(prompts, context, HEAD_SIZE),
        value_cache.reshape(prompts, context, HEAD_SIZE),
        lengths.reshape(1, rows),
        assign.reshape(1, rows),
        jnp.asarray(freq),
    )


def solution(mesh):
    return jax.shard_map(
        functools.partial(local, mesh.shape["tp"]),
        mesh=mesh,
        in_specs=(
            P("grp", "tp"),
            P(("grp", "tp"), None),
            P(None, ("grp", "tp")),
            P("grp", None, "tp", None),
            P("grp", None, "tp", None),
            P("grp"),
            P("grp"),
        ),
        out_specs=P("grp", "tp"),
        check_vma=False,
    )
```

```python
import functools

import jax
import jax.numpy as jnp
import numpy as np
from jax import lax
from jax.experimental import pallas as pl
from jax.experimental.pallas import tpu as pltpu
from jax.sharding import PartitionSpec as P

HEAD_SIZE = 128
PER_KEY = 8
SAMPLES = 8
EPS = 1e-06
ROPE_BASE = 1000000.0
MESH = pl.DeviceIdType.MESH
LOG2E = 1.4426950408889634
MASKED = -1e30
CHUNK = 512
P_TYPE = jnp.bfloat16
Y_TYPE = jnp.bfloat16

NN = (((1,), (0,)), ((), ()))
NT = (((1,), (1,)), ((), ()))


def dot(a, b, dims=NN):
    return lax.dot_general(a, b, dims, preferred_element_type=jnp.float32)


def layer_kernel(
    size, width, x_hbm, w_ref, wo_ref, k_ref, v_ref, len_hbm, assign_hbm, freq_hbm, out_ref,
    x_ref, len_ref, assign_ref, freq_ref,
    xsort, xgot, xbuf, ranks_sum, rows_scale, wbuf, wall, obuf, oall, pbuf, prec, pown, kbuf, vbuf, qs, fresh, lens_sorted, scores,
    mall, ybuf, yrec, yown, zbuf, zrec,
    local_sem, s_send, s_recv, r_send, r_recv, x_send, x_recv, w_send, w_recv, wf_send, wf_recv, o_send, o_recv, of_send, of_recv,
    p_send, p_recv, m_send, m_recv, y_send, y_recv, z_send, z_recv,
):
    g = lax.axis_index("grp")
    t = lax.axis_index("tp")
    q, c = g // 2, g % 2
    rows = x_ref.shape[0]
    head_cols = (PER_KEY + 2) * HEAD_SIZE
    mixed_cols = PER_KEY * HEAD_SIZE
    piece = w_ref.shape[0]
    context = k_ref.shape[1]
    pairs = k_ref.shape[0] // 2

    sibling = (q * 2 + 1 - c, t)

    def summing_rank(chip):
        return chip % (size // 2) * 2 + chip // (size // 2)

    summed_chip = t % 2 * (size // 2) + t // 2
    alone = (summed_chip == q) & (q == t)

    def turn(value, k):
        return lax.rem(value + k, size)

    def rank_device(rank):
        return (g, rank)

    def chip_device(chip):
        return (chip * 2 + c, t)

    side = size // 2

    def across(value):
        return turn(value, side)

    def along(value, k):
        return value // side * side + lax.rem(lax.rem(value, side) + k, side)

    def remote(src, dst, send, recv, device):
        return pltpu.make_async_remote_copy(
            src_ref=src, dst_ref=dst, send_sem=send, recv_sem=recv, device_id=device, device_id_type=MESH
        )

    def await_into(ref, sem):
        pltpu.make_async_copy(ref, ref, sem).wait()

    barrier = pltpu.get_barrier_semaphore()

    def greet(device):
        pl.semaphore_signal(barrier, inc=1, device_id=device, device_id_type=MESH)

    for k in range(1, size):
        greet(rank_device(turn(t, k)))
        greet(chip_device(turn(q, k)))
        greet((t * 2 + c, turn(t, k)))
        greet((turn(q, k) * 2 + c, q))
    greet(sibling)

    @pl.when(q != t)
    def _():
        greet((t * 2 + c, t))
        greet((q * 2 + c, q))

    small = [
        pltpu.make_async_copy(source, goal, local_sem.at[2 + i])
        for i, (source, goal) in enumerate(
            [(assign_hbm, assign_ref), (x_hbm, x_ref), (len_hbm, len_ref), (freq_hbm, freq_ref)]
        )
    ]
    for copy in small:
        copy.start()
    k_copy = pltpu.make_async_copy(k_ref, kbuf, local_sem.at[0])
    v_copy = pltpu.make_async_copy(v_ref, vbuf, local_sem.at[1])
    k_copy.start()
    v_copy.start()

    for copy in small:
        copy.wait()

    assign_row = jnp.broadcast_to(assign_ref[...], (rows, rows))
    i_row = lax.broadcasted_iota(jnp.int32, (rows, rows), 0)
    i_col = lax.broadcasted_iota(jnp.int32, (rows, rows), 1)
    diagonal = i_row == i_col

    def column(row_values):
        return jnp.sum(jnp.where(diagonal, row_values, 0.0), axis=1, keepdims=True)

    assign_f = assign_row.astype(jnp.float32)
    same = assign_f == column(assign_f)
    earlier = jnp.sum(jnp.where(same, jnp.where(i_row < i_col, 1.0, 0.0), 0.0), axis=0, keepdims=True)
    place_row = assign_f * SAMPLES + earlier
    place_col = column(place_row)
    sort_mat = jnp.where(i_row.astype(jnp.float32) == place_row, 1.0, 0.0)
    back_mat = jnp.where(i_col.astype(jnp.float32) == place_col, 1.0, 0.0).astype(jnp.bfloat16)
    lens = jnp.sum(sort_mat * len_ref[...].astype(jnp.float32), axis=1, keepdims=True)
    lens_sorted[...] = jnp.broadcast_to(lens, (rows, HEAD_SIZE))
    sort_mat = sort_mat.astype(jnp.bfloat16)

    xsort[...] = dot(sort_mat, x_ref[...]).astype(jnp.bfloat16)

    lane_diagonal = lax.broadcasted_iota(jnp.int32, (rows, HEAD_SIZE), 0) == lax.broadcasted_iota(
        jnp.int32, (rows, HEAD_SIZE), 1
    )

    features = xsort[...].astype(jnp.float32)
    squares = jnp.sum(features * features, axis=-1, keepdims=True)
    ranks_sum[t] = jnp.broadcast_to(
        jnp.sum(jnp.where(lane_diagonal, squares, 0.0), axis=0, keepdims=True), (8, HEAD_SIZE)
    )

    pl.semaphore_wait(barrier, jnp.where(q == t, 4 * size - 3, 4 * size - 1))

    part_cols = head_cols // 2

    def w_cols(part, rank):
        return pl.ds(pl.multiple_of(rank * head_cols + part * part_cols, HEAD_SIZE), part_cols)

    def w_copy(part, k):
        rank = turn(t, k)
        return remote(
            w_ref.at[:, w_cols(part, rank)], wbuf.at[part, c, t], w_send.at[part, k], w_recv.at[part, t], rank_device(rank)
        )

    def o_copy(k):
        cols = pl.ds(pl.multiple_of(turn(t, k) * mixed_cols, HEAD_SIZE), mixed_cols)
        return remote(wo_ref.at[:, cols], obuf.at[c, t], o_send.at[k], o_recv.at[t], rank_device(turn(t, k)))

    def own_w(part):
        return pltpu.make_async_copy(w_ref.at[:, w_cols(part, t)], wbuf.at[part, c, t], w_recv.at[part, t])

    own_mixed = pl.ds(pl.multiple_of(t * mixed_cols, HEAD_SIZE), mixed_cols)
    own_o = pltpu.make_async_copy(wo_ref.at[:, own_mixed], obuf.at[c, t], o_recv.at[t])

    def x_copy(k):
        return remote(xsort, xgot.at[q], x_send.at[k], x_recv.at[q], (t * 2 + c, turn(t, k)))

    own_x = pltpu.make_async_copy(xsort, xgot.at[q], x_recv.at[q])

    @pl.when(q == t)
    def _():
        own_x.start()

    @pl.when(q != t)
    def _():
        x_copy(0).start()

    for k in range(1, size):
        x_copy(k).start()

    def s_copy(k):
        return remote(ranks_sum.at[t], ranks_sum.at[t], s_send.at[k], s_recv.at[t], rank_device(turn(t, k)))

    def r_copy(k):
        return remote(rows_scale.at[q], rows_scale.at[q], r_send.at[k], r_recv.at[q], chip_device(turn(q, k)))

    for k in range(1, size):
        s_copy(k).start()

    for part in range(2):
        own_w(part).start()
        for k in range(1, size):
            w_copy(part, k).start()
    own_o.start()

    angle = lens * freq_ref[...]
    lane = lax.broadcasted_iota(jnp.int32, (rows, HEAD_SIZE), 1)
    cosine = jnp.cos(angle)
    sine = jnp.where(lane < HEAD_SIZE // 2, -1.0, 1.0) * jnp.sin(angle)

    for k in range(1, size):
        await_into(ranks_sum.at[turn(t, k)], s_recv.at[turn(t, k)])
    total = ranks_sum[0]
    for s in range(1, size):
        total = total + ranks_sum[s]
    rows_scale[q] = lax.rsqrt(total * (1.0 / width) + EPS)
    for k in range(1, size):
        r_copy(k).start()

    def wf_copy(part, s):
        piece_at = wbuf.at[part, c, s]
        return remote(piece_at, piece_at, wf_send.at[part, s], wf_recv.at[part, s], sibling)

    def of_copy(s):
        return remote(obuf.at[c, s], obuf.at[c, s], of_send.at[s], of_recv.at[s], sibling)

    def norm_rows():
        for k in range(1, size):
            await_into(rows_scale.at[turn(q, k)], r_recv.at[turn(q, k)])
        for chip in range(size):
            await_into(xgot.at[chip], x_recv.at[chip])
            scale = jnp.sum(jnp.where(lane_diagonal, rows_scale[chip, :1], 0.0), axis=1, keepdims=True)
            xbuf[chip] = (xgot[chip].astype(jnp.float32) * scale).astype(jnp.bfloat16)

    def gather_weights(part):
        for k in range(size):
            s = turn(t, size - k)
            await_into(wbuf.at[part, c, s], w_recv.at[part, s])
            wf_copy(part, s).start()
        if part == 0:
            norm_rows()
        for s in range(size):
            await_into(wbuf.at[part, 1 - c, s], wf_recv.at[part, s])
        for core in range(2):
            for s in range(size):
                first = (core * size + s) * piece
                wall[part, first : first + piece, :] = wbuf[part, core, s]

    gather_weights(0)

    half_rows = rows // 2
    halves = [slice(half * half_rows, (half + 1) * half_rows) for half in range(2)]

    def p_copy(part, half, chip):
        return remote(
            pbuf.at[part, half, chip],
            prec.at[part, half, q],
            p_send.at[part, half, chip],
            p_recv.at[part, half, q],
            chip_device(chip),
        )

    def project(part, half):
        block = dot(xbuf[:, halves[half], :].reshape(size * half_rows, -1), wall[part])
        for chip in range(size):
            result = block[chip * half_rows : (chip + 1) * half_rows]

            @pl.when(chip == q)
            def _():
                pown[part, half] = result

            @pl.when(chip != q)
            def _():
                pbuf[part, half, chip] = result.astype(pbuf.dtype)
                p_copy(part, half, chip).start()

    project(0, 0)
    gather_weights(1)
    project(1, 0)
    project(0, 1)
    project(1, 1)

    def prepare(half):
        for k in range(1, size):
            for part in range(2):
                await_into(prec.at[part, half, turn(q, k)], p_recv.at[part, half, turn(q, k)])
        for h in range(PER_KEY + 2):
            part, place = divmod(h, (PER_KEY + 2) // 2)
            cols = slice(place * HEAD_SIZE, (place + 1) * HEAD_SIZE)
            head = pown[part, half, :, cols]
            for k in range(1, size):
                head = head + prec[part, half, turn(q, k), :, cols].astype(jnp.float32)
            if h <= PER_KEY:
                head = head * lax.rsqrt(jnp.mean(head * head, axis=-1, keepdims=True) + EPS)
                rolled = pltpu.roll(head, HEAD_SIZE // 2, 1)
                head = head * cosine[halves[half]] + rolled * sine[halves[half]]
            head = head.astype(jnp.bfloat16).astype(jnp.float32)
            if h < PER_KEY:
                qs[h, halves[half], :] = head
            else:
                fresh[h - PER_KEY, halves[half], :] = head

    scale2 = HEAD_SIZE ** (-0.5) * LOG2E
    queries = PER_KEY * SAMPLES
    slot_iota = lax.broadcasted_iota(jnp.int32, (queries, HEAD_SIZE), 1).astype(jnp.float32)

    def attend(p):
        mine = pl.ds(pl.multiple_of(p * SAMPLES, SAMPLES), SAMPLES)
        query = qs[:, mine, :]
        own = jnp.sum(query * fresh[0, mine, :][None], axis=-1, keepdims=True).reshape(queries, 1)
        fresh_value = jnp.broadcast_to(fresh[1, mine, :][None], query.shape).reshape(queries, HEAD_SIZE)
        seen = jnp.broadcast_to(lens_sorted[mine, :][None], query.shape).reshape(queries, HEAD_SIZE)
        query = query.reshape(queries, HEAD_SIZE).astype(jnp.bfloat16)
        top = jnp.full((queries, HEAD_SIZE), MASKED, jnp.float32)
        for chunk in range(context // CHUNK):
            part = dot(query, kbuf[p, chunk * CHUNK : (chunk + 1) * CHUNK, :], NT)
            for lane in range(CHUNK // HEAD_SIZE):
                first = chunk * CHUNK + lane * HEAD_SIZE
                tile = part[:, lane * HEAD_SIZE : (lane + 1) * HEAD_SIZE]
                tile = jnp.where(slot_iota < seen - first, tile, MASKED)
                scores[:, first : first + HEAD_SIZE] = tile
                top = jnp.maximum(top, tile)
        peak = jnp.maximum(jnp.max(top, axis=-1, keepdims=True), own)
        shift = peak * scale2
        own_weight = jnp.exp2(own * scale2 - shift)
        sums = jnp.zeros((queries, HEAD_SIZE), jnp.float32)
        for chunk in range(context // CHUNK):
            cols = slice(chunk * CHUNK, (chunk + 1) * CHUNK)
            weights = jnp.exp2(scores[:, cols] * scale2 - shift)
            scores[:, cols] = weights
            for lane in range(CHUNK // HEAD_SIZE):
                sums = sums + weights[:, lane * HEAD_SIZE : (lane + 1) * HEAD_SIZE]
        part = 1.0 / (jnp.sum(sums, axis=-1, keepdims=True) + own_weight)
        mixed = (own_weight * part).astype(jnp.bfloat16).astype(jnp.float32) * fresh_value
        for chunk in range(context // CHUNK):
            cols = slice(chunk * CHUNK, (chunk + 1) * CHUNK)
            mixed = mixed + dot((scores[:, cols] * part).astype(jnp.bfloat16), vbuf[p, cols, :])
        return mixed

    def m_copy(i, source, chip, sem):
        return remote(
            mall.at[source, i], mall.at[source, i], m_send.at[i, sem], m_recv.at[i, source], chip_device(chip)
        )

    def m_across(i):
        return m_copy(i, q, across(q), 0)

    def m_own(i, k):
        return m_copy(i, q, along(q, k), k)

    def m_passed(i, k):
        return m_copy(i, across(q), along(q, k), side + k)

    def pass_on(i):
        await_into(mall.at[across(q), i], m_recv.at[i, across(q)])
        for k in range(1, side):
            m_passed(i, k).start()

    def attend_pair(i):
        low, high = attend(2 * i), attend(2 * i + 1)
        for h in range(PER_KEY):
            part = slice(h * SAMPLES, (h + 1) * SAMPLES)
            mall[q, i, :, h * HEAD_SIZE : (h + 1) * HEAD_SIZE] = jnp.concatenate(
                [low[part], high[part]], axis=0
            ).astype(jnp.bfloat16)

    prepare(0)
    k_copy.wait()
    v_copy.wait()
    for i in range(pairs):
        if i == 1:
            for k in range(1, size):
                o_copy(k).start()
        if i == pairs // 2:
            prepare(1)
        if i == pairs - 1:
            for s in range(size):
                await_into(obuf.at[c, s], o_recv.at[s])
                of_copy(s).start()
        attend_pair(i)
        m_across(i).start()
        for k in range(1, side):
            m_own(i, k).start()
        if i > 0:
            pass_on(i - 1)
    pass_on(pairs - 1)
    for s in range(size):
        await_into(obuf.at[1 - c, s], of_recv.at[s])
    for core in range(2):
        for s in range(size):
            first = (core * size + s) * piece
            oall[first : first + piece, :] = obuf[core, s]

    def y_copy(half, rank):
        return remote(
            ybuf.at[half, rank], yrec.at[half, t], y_send.at[half, rank], y_recv.at[half, t], rank_device(rank)
        )

    half_pairs = pairs // 2

    def project_out(half):
        for chip in range(size):
            for i in range(half * half_pairs, (half + 1) * half_pairs):

                @pl.when((chip != q) & (chip != across(q)))
                def _():
                    await_into(mall.at[chip, i], m_recv.at[i, chip])

        block = mall[:, half * half_pairs : (half + 1) * half_pairs].reshape(size * half_rows, mixed_cols)
        block = dot(block, oall[...], NT)
        for chip in range(size):
            rank = summing_rank(chip)
            result = block[chip * half_rows : (chip + 1) * half_rows]

            @pl.when(rank == t)
            def _():
                yown[half] = result

            @pl.when(rank != t)
            def _():
                ybuf[half, rank] = result.astype(ybuf.dtype)
                y_copy(half, rank).start()

    def z_copy(half):
        return remote(zbuf.at[half], zrec.at[half], z_send.at[half], z_recv.at[half], (summed_chip * 2 + c, q))

    project_out(0)
    project_out(1)
    for half in range(2):
        result = yown[half]
        for k in range(1, size):
            await_into(yrec.at[half, turn(t, k)], y_recv.at[half, turn(t, k)])
        for k in range(1, size):
            result = result + yrec[half, turn(t, k)].astype(jnp.float32)
        zbuf[half] = result.astype(jnp.bfloat16)

        @pl.when(jnp.logical_not(alone))
        def _():
            z_copy(half).start()

    @pl.when(jnp.logical_not(alone))
    def _():
        for half in range(2):
            z_copy(half).wait()

    @pl.when(alone)
    def _():
        zrec[...] = zbuf[...]

    out_ref[...] = dot(back_mat, zrec[...].reshape(rows, -1)).astype(jnp.bfloat16)

    @pl.when(q != t)
    def _():
        x_copy(0).wait_send()

    for k in range(1, size):
        x_copy(k).wait_send()
        s_copy(k).wait_send()
        r_copy(k).wait_send()
        for part in range(2):
            w_copy(part, k).wait_send()
        o_copy(k).wait_send()
        for half in range(2):
            for part in range(2):
                p_copy(part, half, turn(q, k)).wait_send()
            y_copy(half, turn(t, k)).wait_send()
    for i in range(pairs):
        m_across(i).wait_send()
        for k in range(1, side):
            m_own(i, k).wait_send()
            m_passed(i, k).wait_send()
    for s in range(size):
        for part in range(2):
            wf_copy(part, s).wait_send()
        of_copy(s).wait_send()


def local(size, hidden, query_key_value_weight, w_out, k_cache, value_cache, lengths, assign):
    rows, features = hidden.shape
    width = features * size
    piece = query_key_value_weight.shape[0]
    prompts, context = k_cache.shape[0], k_cache.shape[1]
    half = np.arange(HEAD_SIZE // 2, dtype=np.float32)
    freq = np.float32(ROPE_BASE) ** (-half * np.float32(2.0) / np.float32(HEAD_SIZE))
    freq = np.concatenate([freq, freq]).astype(np.float32)[None, :]
    head_cols = (PER_KEY + 2) * HEAD_SIZE
    mixed_cols = PER_KEY * HEAD_SIZE
    bf16, f32 = jnp.bfloat16, jnp.float32
    dma = pltpu.SemaphoreType.DMA
    pairs = prompts // 2
    vmem = pl.BlockSpec(memory_space=pltpu.VMEM)
    anywhere = pl.BlockSpec(memory_space=pl.ANY)
    return pl.pallas_call(
        functools.partial(layer_kernel, size, width),
        out_shape=jax.ShapeDtypeStruct((rows, features), bf16),
        in_specs=[anywhere] * 8,
        out_specs=vmem,
        scratch_shapes=[
            pltpu.VMEM((rows, features), bf16),
            pltpu.VMEM((1, rows), jnp.int32),
            pltpu.VMEM((1, rows), jnp.int32),
            pltpu.VMEM((1, HEAD_SIZE), f32),
            pltpu.VMEM((rows, features), bf16),
            pltpu.VMEM((size, rows, features), bf16),
            pltpu.VMEM((size, rows, features), bf16),
            pltpu.VMEM((size, 8, HEAD_SIZE), f32),
            pltpu.VMEM((size, 8, HEAD_SIZE), f32),
            pltpu.VMEM((2, 2, size, piece, head_cols // 2), bf16),
            pltpu.VMEM((2, features, head_cols // 2), bf16),
            pltpu.VMEM((2, size, piece, mixed_cols), bf16),
            pltpu.VMEM((features, mixed_cols), bf16),
            pltpu.VMEM((2, 2, size, rows // 2, head_cols // 2), P_TYPE),
            pltpu.VMEM((2, 2, size, rows // 2, head_cols // 2), P_TYPE),
            pltpu.VMEM((2, 2, rows // 2, head_cols // 2), f32),
            pltpu.VMEM((prompts, context, HEAD_SIZE), bf16),
            pltpu.VMEM((prompts, context, HEAD_SIZE), bf16),
            pltpu.VMEM((PER_KEY, rows, HEAD_SIZE), f32),
            pltpu.VMEM((2, rows, HEAD_SIZE), f32),
            pltpu.VMEM((rows, HEAD_SIZE), f32),
            pltpu.VMEM((PER_KEY * SAMPLES, context), f32),
            pltpu.VMEM((size, pairs, 2 * SAMPLES, mixed_cols), bf16),
            pltpu.VMEM((2, size, rows // 2, features), Y_TYPE),
            pltpu.VMEM((2, size, rows // 2, features), Y_TYPE),
            pltpu.VMEM((2, rows // 2, features), f32),
            pltpu.VMEM((2, rows // 2, features), bf16),
            pltpu.VMEM((2, rows // 2, features), bf16),
            dma((6,)),
            dma((size,)), dma((size,)), dma((size,)), dma((size,)),
            dma((size,)), dma((size,)),
            dma((2, size)), dma((2, size)), dma((2, size)), dma((2, size)),
            dma((size,)), dma((size,)), dma((size,)), dma((size,)),
            dma((2, 2, size)), dma((2, 2, size)),
            dma((pairs, size)), dma((pairs, size)),
            dma((2, size)), dma((2, size)),
            dma((2,)), dma((2,)),
        ],
        compiler_params=pltpu.CompilerParams(
            collective_id=0, has_side_effects=True, vmem_limit_bytes=56 * 1024 * 1024
        ),
        name="layer",
    )(
        hidden,
        query_key_value_weight,
        w_out.T,
        k_cache.reshape(prompts, context, HEAD_SIZE),
        value_cache.reshape(prompts, context, HEAD_SIZE),
        lengths.reshape(1, rows),
        assign.reshape(1, rows),
        jnp.asarray(freq),
    )


def solution(mesh):
    return jax.shard_map(
        functools.partial(local, mesh.shape["tp"]),
        mesh=mesh,
        in_specs=(
            P("grp", "tp"),
            P(("grp", "tp"), None),
            P(None, ("grp", "tp")),
            P("grp", None, "tp", None),
            P("grp", None, "tp", None),
            P("grp"),
            P("grp"),
        ),
        out_specs=P("grp", "tp"),
        check_vma=False,
    )
```

```python
import functools

import jax
import jax.numpy as jnp
import numpy as np
from jax import lax
from jax.experimental import pallas as pl
from jax.experimental.pallas import tpu as pltpu
from jax.sharding import PartitionSpec as P

HEAD_SIZE = 128
PER_KEY = 8
SAMPLES = 8
EPS = 1e-06
ROPE_BASE = 1000000.0
MESH = pl.DeviceIdType.MESH
LOG2E = 1.4426950408889634
MASKED = -1e30
CHUNK = 512
P_TYPE = jnp.bfloat16
Y_TYPE = jnp.bfloat16

NN = (((1,), (0,)), ((), ()))
NT = (((1,), (1,)), ((), ()))


def dot(a, b, dims=NN):
    return lax.dot_general(a, b, dims, preferred_element_type=jnp.float32)


def layer_kernel(
    size, width, x_hbm, w_ref, wo_ref, k_ref, v_ref, len_hbm, assign_hbm, freq_hbm, out_ref,
    x_ref, len_ref, assign_ref, freq_ref,
    xsort, xgot, xbuf, ranks_sum, rows_scale, wbuf, wall, obuf, oall, pbuf, prec, pown, kbuf, vbuf, qs, fresh, lens_sorted, scores,
    mall, ybuf, yrec, yown, zbuf, zrec,
    local_sem, s_send, s_recv, r_send, r_recv, x_send, x_recv, w_send, w_recv, wf_send, wf_recv, o_send, o_recv, of_send, of_recv,
    p_send, p_recv, m_send, m_recv, y_send, y_recv, z_send, z_recv,
):
    g = lax.axis_index("grp")
    t = lax.axis_index("tp")
    q, c = g // 2, g % 2
    rows = x_ref.shape[0]
    head_cols = (PER_KEY + 2) * HEAD_SIZE
    mixed_cols = PER_KEY * HEAD_SIZE
    piece = w_ref.shape[0]
    context = k_ref.shape[1]
    pairs = k_ref.shape[0] // 2

    sibling = (q * 2 + 1 - c, t)

    def summing_rank(chip):
        return chip % (size // 2) * 2 + chip // (size // 2)

    summed_chip = t % 2 * (size // 2) + t // 2
    alone = (summed_chip == q) & (q == t)

    def turn(value, k):
        return lax.rem(value + k, size)

    def rank_device(rank):
        return (g, rank)

    def chip_device(chip):
        return (chip * 2 + c, t)

    side = size // 2

    def across(value):
        return turn(value, side)

    def along(value, k):
        return value // side * side + lax.rem(lax.rem(value, side) + k, side)

    def remote(src, dst, send, recv, device):
        return pltpu.make_async_remote_copy(
            src_ref=src, dst_ref=dst, send_sem=send, recv_sem=recv, device_id=device, device_id_type=MESH
        )

    def await_into(ref, sem):
        pltpu.make_async_copy(ref, ref, sem).wait()

    barrier = pltpu.get_barrier_semaphore()

    def greet(device):
        pl.semaphore_signal(barrier, inc=1, device_id=device, device_id_type=MESH)

    for k in range(1, size):
        greet(rank_device(turn(t, k)))
        greet(chip_device(turn(q, k)))
        greet((t * 2 + c, turn(t, k)))
        greet((turn(q, k) * 2 + c, q))
    greet(sibling)

    @pl.when(q != t)
    def _():
        greet((t * 2 + c, t))
        greet((q * 2 + c, q))

    small = [
        pltpu.make_async_copy(source, goal, local_sem.at[2 + i])
        for i, (source, goal) in enumerate(
            [(assign_hbm, assign_ref), (x_hbm, x_ref), (len_hbm, len_ref), (freq_hbm, freq_ref)]
        )
    ]
    for copy in small:
        copy.start()
    k_copy = pltpu.make_async_copy(k_ref, kbuf, local_sem.at[0])
    v_copy = pltpu.make_async_copy(v_ref, vbuf, local_sem.at[1])
    k_copy.start()
    v_copy.start()

    for copy in small:
        copy.wait()

    assign_row = jnp.broadcast_to(assign_ref[...], (rows, rows))
    i_row = lax.broadcasted_iota(jnp.int32, (rows, rows), 0)
    i_col = lax.broadcasted_iota(jnp.int32, (rows, rows), 1)
    diagonal = i_row == i_col

    def column(row_values):
        return jnp.sum(jnp.where(diagonal, row_values, 0.0), axis=1, keepdims=True)

    assign_f = assign_row.astype(jnp.float32)
    same = assign_f == column(assign_f)
    earlier = jnp.sum(jnp.where(same, jnp.where(i_row < i_col, 1.0, 0.0), 0.0), axis=0, keepdims=True)
    place_row = assign_f * SAMPLES + earlier
    sort_mat = jnp.where(i_row.astype(jnp.float32) == place_row, 1.0, 0.0)
    lens = jnp.sum(sort_mat * len_ref[...].astype(jnp.float32), axis=1, keepdims=True)
    lens_sorted[...] = jnp.broadcast_to(lens, (rows, HEAD_SIZE))
    sort_mat = sort_mat.astype(jnp.bfloat16)

    xsort[...] = dot(sort_mat, x_ref[...]).astype(jnp.bfloat16)

    lane_diagonal = lax.broadcasted_iota(jnp.int32, (rows, HEAD_SIZE), 0) == lax.broadcasted_iota(
        jnp.int32, (rows, HEAD_SIZE), 1
    )

    features = xsort[...].astype(jnp.float32)
    squares = jnp.sum(features * features, axis=-1, keepdims=True)
    ranks_sum[t] = jnp.broadcast_to(
        jnp.sum(jnp.where(lane_diagonal, squares, 0.0), axis=0, keepdims=True), (8, HEAD_SIZE)
    )

    pl.semaphore_wait(barrier, jnp.where(q == t, 4 * size - 3, 4 * size - 1))

    part_cols = head_cols // 2

    def w_cols(part, rank):
        return pl.ds(pl.multiple_of(rank * head_cols + part * part_cols, HEAD_SIZE), part_cols)

    def w_copy(part, k):
        rank = turn(t, k)
        return remote(
            w_ref.at[:, w_cols(part, rank)], wbuf.at[part, c, t], w_send.at[part, k], w_recv.at[part, t], rank_device(rank)
        )

    def o_copy(k):
        cols = pl.ds(pl.multiple_of(turn(t, k) * mixed_cols, HEAD_SIZE), mixed_cols)
        return remote(wo_ref.at[:, cols], obuf.at[c, t], o_send.at[k], o_recv.at[t], rank_device(turn(t, k)))

    def own_w(part):
        return pltpu.make_async_copy(w_ref.at[:, w_cols(part, t)], wbuf.at[part, c, t], w_recv.at[part, t])

    own_mixed = pl.ds(pl.multiple_of(t * mixed_cols, HEAD_SIZE), mixed_cols)
    own_o = pltpu.make_async_copy(wo_ref.at[:, own_mixed], obuf.at[c, t], o_recv.at[t])

    def x_copy(k):
        return remote(xsort, xgot.at[q], x_send.at[k], x_recv.at[q], (t * 2 + c, turn(t, k)))

    own_x = pltpu.make_async_copy(xsort, xgot.at[q], x_recv.at[q])

    @pl.when(q == t)
    def _():
        own_x.start()

    @pl.when(q != t)
    def _():
        x_copy(0).start()

    for k in range(1, size):
        x_copy(k).start()

    def s_copy(k):
        return remote(ranks_sum.at[t], ranks_sum.at[t], s_send.at[k], s_recv.at[t], rank_device(turn(t, k)))

    def r_copy(k):
        return remote(rows_scale.at[q], rows_scale.at[q], r_send.at[k], r_recv.at[q], chip_device(turn(q, k)))

    for k in range(1, size):
        s_copy(k).start()

    for part in range(2):
        own_w(part).start()
        for k in range(1, size):
            w_copy(part, k).start()
    own_o.start()

    angle = lens * freq_ref[...]
    lane = lax.broadcasted_iota(jnp.int32, (rows, HEAD_SIZE), 1)
    cosine = jnp.cos(angle)
    sine = jnp.where(lane < HEAD_SIZE // 2, -1.0, 1.0) * jnp.sin(angle)

    for k in range(1, size):
        await_into(ranks_sum.at[turn(t, k)], s_recv.at[turn(t, k)])
    total = ranks_sum[0]
    for s in range(1, size):
        total = total + ranks_sum[s]
    rows_scale[q] = lax.rsqrt(total * (1.0 / width) + EPS)
    for k in range(1, size):
        r_copy(k).start()

    def wf_copy(part, s):
        piece_at = wbuf.at[part, c, s]
        return remote(piece_at, piece_at, wf_send.at[part, s], wf_recv.at[part, s], sibling)

    def of_copy(s):
        return remote(obuf.at[c, s], obuf.at[c, s], of_send.at[s], of_recv.at[s], sibling)

    def norm_rows():
        for k in range(1, size):
            await_into(rows_scale.at[turn(q, k)], r_recv.at[turn(q, k)])
        for chip in range(size):
            await_into(xgot.at[chip], x_recv.at[chip])
            scale = jnp.sum(jnp.where(lane_diagonal, rows_scale[chip, :1], 0.0), axis=1, keepdims=True)
            xbuf[chip] = (xgot[chip].astype(jnp.float32) * scale).astype(jnp.bfloat16)

    def gather_weights(part):
        for k in range(size):
            s = turn(t, size - k)
            await_into(wbuf.at[part, c, s], w_recv.at[part, s])
            wf_copy(part, s).start()
        if part == 0:
            norm_rows()
        for s in range(size):
            await_into(wbuf.at[part, 1 - c, s], wf_recv.at[part, s])
        for core in range(2):
            for s in range(size):
                first = (core * size + s) * piece
                wall[part, first : first + piece, :] = wbuf[part, core, s]

    gather_weights(0)

    half_rows = rows // 2
    halves = [slice(half * half_rows, (half + 1) * half_rows) for half in range(2)]

    def p_copy(part, half, chip):
        return remote(
            pbuf.at[part, half, chip],
            prec.at[part, half, q],
            p_send.at[part, half, chip],
            p_recv.at[part, half, q],
            chip_device(chip),
        )

    def project(part, half):
        block = dot(xbuf[:, halves[half], :].reshape(size * half_rows, -1), wall[part])
        for chip in range(size):
            result = block[chip * half_rows : (chip + 1) * half_rows]

            @pl.when(chip == q)
            def _():
                pown[part, half] = result

            @pl.when(chip != q)
            def _():
                pbuf[part, half, chip] = result.astype(pbuf.dtype)
                p_copy(part, half, chip).start()

    project(0, 0)
    gather_weights(1)
    project(1, 0)
    project(0, 1)
    project(1, 1)

    def prepare(half):
        for k in range(1, size):
            for part in range(2):
                await_into(prec.at[part, half, turn(q, k)], p_recv.at[part, half, turn(q, k)])
        for h in range(PER_KEY + 2):
            part, place = divmod(h, (PER_KEY + 2) // 2)
            cols = slice(place * HEAD_SIZE, (place + 1) * HEAD_SIZE)
            head = pown[part, half, :, cols]
            for k in range(1, size):
                head = head + prec[part, half, turn(q, k), :, cols].astype(jnp.float32)
            if h <= PER_KEY:
                head = head * lax.rsqrt(jnp.mean(head * head, axis=-1, keepdims=True) + EPS)
                rolled = pltpu.roll(head, HEAD_SIZE // 2, 1)
                head = head * cosine[halves[half]] + rolled * sine[halves[half]]
            head = head.astype(jnp.bfloat16).astype(jnp.float32)
            if h < PER_KEY:
                qs[h, halves[half], :] = head
            else:
                fresh[h - PER_KEY, halves[half], :] = head

    scale2 = HEAD_SIZE ** (-0.5) * LOG2E
    queries = PER_KEY * SAMPLES
    slot_iota = lax.broadcasted_iota(jnp.int32, (queries, HEAD_SIZE), 1).astype(jnp.float32)

    def attend(p):
        mine = pl.ds(pl.multiple_of(p * SAMPLES, SAMPLES), SAMPLES)
        query = qs[:, mine, :]
        own = jnp.sum(query * fresh[0, mine, :][None], axis=-1, keepdims=True).reshape(queries, 1)
        fresh_value = jnp.broadcast_to(fresh[1, mine, :][None], query.shape).reshape(queries, HEAD_SIZE)
        seen = jnp.broadcast_to(lens_sorted[mine, :][None], query.shape).reshape(queries, HEAD_SIZE)
        query = query.reshape(queries, HEAD_SIZE).astype(jnp.bfloat16)
        top = jnp.full((queries, HEAD_SIZE), MASKED, jnp.float32)
        for chunk in range(context // CHUNK):
            part = dot(query, kbuf[p, chunk * CHUNK : (chunk + 1) * CHUNK, :], NT)
            for lane in range(CHUNK // HEAD_SIZE):
                first = chunk * CHUNK + lane * HEAD_SIZE
                tile = part[:, lane * HEAD_SIZE : (lane + 1) * HEAD_SIZE]
                tile = jnp.where(slot_iota < seen - first, tile, MASKED)
                scores[:, first : first + HEAD_SIZE] = tile
                top = jnp.maximum(top, tile)
        peak = jnp.maximum(jnp.max(top, axis=-1, keepdims=True), own)
        shift = peak * scale2
        own_weight = jnp.exp2(own * scale2 - shift)
        sums = jnp.zeros((queries, HEAD_SIZE), jnp.float32)
        for chunk in range(context // CHUNK):
            cols = slice(chunk * CHUNK, (chunk + 1) * CHUNK)
            weights = jnp.exp2(scores[:, cols] * scale2 - shift)
            scores[:, cols] = weights
            for lane in range(CHUNK // HEAD_SIZE):
                sums = sums + weights[:, lane * HEAD_SIZE : (lane + 1) * HEAD_SIZE]
        part = 1.0 / (jnp.sum(sums, axis=-1, keepdims=True) + own_weight)
        mixed = (own_weight * part).astype(jnp.bfloat16).astype(jnp.float32) * fresh_value
        for chunk in range(context // CHUNK):
            cols = slice(chunk * CHUNK, (chunk + 1) * CHUNK)
            mixed = mixed + dot((scores[:, cols] * part).astype(jnp.bfloat16), vbuf[p, cols, :])
        return mixed

    def m_copy(i, source, chip, sem):
        return remote(
            mall.at[source, i], mall.at[source, i], m_send.at[i, sem], m_recv.at[i, source], chip_device(chip)
        )

    def m_across(i):
        return m_copy(i, q, across(q), 0)

    def m_own(i, k):
        return m_copy(i, q, along(q, k), k)

    def m_passed(i, k):
        return m_copy(i, across(q), along(q, k), side + k)

    def pass_on(i):
        await_into(mall.at[across(q), i], m_recv.at[i, across(q)])
        for k in range(1, side):
            m_passed(i, k).start()

    def attend_pair(i):
        low, high = attend(2 * i), attend(2 * i + 1)
        for h in range(PER_KEY):
            part = slice(h * SAMPLES, (h + 1) * SAMPLES)
            mall[q, i, :, h * HEAD_SIZE : (h + 1) * HEAD_SIZE] = jnp.concatenate(
                [low[part], high[part]], axis=0
            ).astype(jnp.bfloat16)

    prepare(0)
    k_copy.wait()
    v_copy.wait()
    for i in range(pairs):
        if i == 1:
            for k in range(1, size):
                o_copy(k).start()
        if i == pairs // 2:
            prepare(1)
        if i == pairs - 1:
            for s in range(size):
                await_into(obuf.at[c, s], o_recv.at[s])
                of_copy(s).start()
        attend_pair(i)
        m_across(i).start()
        for k in range(1, side):
            m_own(i, k).start()
        if i > 0:
            pass_on(i - 1)
    pass_on(pairs - 1)
    for s in range(size):
        await_into(obuf.at[1 - c, s], of_recv.at[s])
    for core in range(2):
        for s in range(size):
            first = (core * size + s) * piece
            oall[first : first + piece, :] = obuf[core, s]

    def y_copy(half, rank):
        return remote(
            ybuf.at[half, rank], yrec.at[half, t], y_send.at[half, rank], y_recv.at[half, t], rank_device(rank)
        )

    half_pairs = pairs // 2

    def project_out(half):
        for chip in range(size):
            for i in range(half * half_pairs, (half + 1) * half_pairs):

                @pl.when((chip != q) & (chip != across(q)))
                def _():
                    await_into(mall.at[chip, i], m_recv.at[i, chip])

        block = mall[:, half * half_pairs : (half + 1) * half_pairs].reshape(size * half_rows, mixed_cols)
        block = dot(block, oall[...], NT)
        for chip in range(size):
            rank = summing_rank(chip)
            result = block[chip * half_rows : (chip + 1) * half_rows]

            @pl.when(rank == t)
            def _():
                yown[half] = result

            @pl.when(rank != t)
            def _():
                ybuf[half, rank] = result.astype(ybuf.dtype)
                y_copy(half, rank).start()

    def z_copy(half):
        return remote(zbuf.at[half], zrec.at[half], z_send.at[half], z_recv.at[half], (summed_chip * 2 + c, q))

    project_out(0)
    project_out(1)
    for half in range(2):
        result = yown[half]
        for k in range(1, size):
            await_into(yrec.at[half, turn(t, k)], y_recv.at[half, turn(t, k)])
        for k in range(1, size):
            result = result + yrec[half, turn(t, k)].astype(jnp.float32)
        zbuf[half] = result.astype(jnp.bfloat16)

        @pl.when(jnp.logical_not(alone))
        def _():
            z_copy(half).start()

    @pl.when(jnp.logical_not(alone))
    def _():
        for half in range(2):
            z_copy(half).wait()

    @pl.when(alone)
    def _():
        zrec[...] = zbuf[...]

    for half in range(2):
        out_ref[halves[half], :] = zrec[half]

    @pl.when(q != t)
    def _():
        x_copy(0).wait_send()

    for k in range(1, size):
        x_copy(k).wait_send()
        s_copy(k).wait_send()
        r_copy(k).wait_send()
        for part in range(2):
            w_copy(part, k).wait_send()
        o_copy(k).wait_send()
        for half in range(2):
            for part in range(2):
                p_copy(part, half, turn(q, k)).wait_send()
            y_copy(half, turn(t, k)).wait_send()
    for i in range(pairs):
        m_across(i).wait_send()
        for k in range(1, side):
            m_own(i, k).wait_send()
            m_passed(i, k).wait_send()
    for s in range(size):
        for part in range(2):
            wf_copy(part, s).wait_send()
        of_copy(s).wait_send()


def restore_kernel(sorted_ref, assign_ref, out_ref):
    rows = sorted_ref.shape[0]
    i_row = lax.broadcasted_iota(jnp.int32, (rows, rows), 0)
    i_col = lax.broadcasted_iota(jnp.int32, (rows, rows), 1)
    row_values = jnp.broadcast_to(assign_ref[...], (rows, rows)).astype(jnp.float32)
    col_values = jnp.sum(jnp.where(i_row == i_col, row_values, 0.0), axis=1, keepdims=True)
    earlier = jnp.where(i_col < i_row, jnp.where(row_values == col_values, 1.0, 0.0), 0.0)
    place = col_values * SAMPLES + jnp.sum(earlier, axis=1, keepdims=True)
    back = jnp.where(i_col.astype(jnp.float32) == place, 1.0, 0.0).astype(jnp.bfloat16)
    out_ref[...] = dot(back, sorted_ref[...]).astype(jnp.bfloat16)


def local(size, hidden, query_key_value_weight, w_out, k_cache, value_cache, lengths, assign):
    rows, features = hidden.shape
    width = features * size
    piece = query_key_value_weight.shape[0]
    prompts, context = k_cache.shape[0], k_cache.shape[1]
    half = np.arange(HEAD_SIZE // 2, dtype=np.float32)
    freq = np.float32(ROPE_BASE) ** (-half * np.float32(2.0) / np.float32(HEAD_SIZE))
    freq = np.concatenate([freq, freq]).astype(np.float32)[None, :]
    head_cols = (PER_KEY + 2) * HEAD_SIZE
    mixed_cols = PER_KEY * HEAD_SIZE
    bf16, f32 = jnp.bfloat16, jnp.float32
    dma = pltpu.SemaphoreType.DMA
    pairs = prompts // 2
    vmem = pl.BlockSpec(memory_space=pltpu.VMEM)
    anywhere = pl.BlockSpec(memory_space=pl.ANY)
    finished = pl.pallas_call(
        functools.partial(layer_kernel, size, width),
        out_shape=jax.ShapeDtypeStruct((rows, features), bf16),
        in_specs=[anywhere] * 8,
        out_specs=vmem,
        scratch_shapes=[
            pltpu.VMEM((rows, features), bf16),
            pltpu.VMEM((1, rows), jnp.int32),
            pltpu.VMEM((1, rows), jnp.int32),
            pltpu.VMEM((1, HEAD_SIZE), f32),
            pltpu.VMEM((rows, features), bf16),
            pltpu.VMEM((size, rows, features), bf16),
            pltpu.VMEM((size, rows, features), bf16),
            pltpu.VMEM((size, 8, HEAD_SIZE), f32),
            pltpu.VMEM((size, 8, HEAD_SIZE), f32),
            pltpu.VMEM((2, 2, size, piece, head_cols // 2), bf16),
            pltpu.VMEM((2, features, head_cols // 2), bf16),
            pltpu.VMEM((2, size, piece, mixed_cols), bf16),
            pltpu.VMEM((features, mixed_cols), bf16),
            pltpu.VMEM((2, 2, size, rows // 2, head_cols // 2), P_TYPE),
            pltpu.VMEM((2, 2, size, rows // 2, head_cols // 2), P_TYPE),
            pltpu.VMEM((2, 2, rows // 2, head_cols // 2), f32),
            pltpu.VMEM((prompts, context, HEAD_SIZE), bf16),
            pltpu.VMEM((prompts, context, HEAD_SIZE), bf16),
            pltpu.VMEM((PER_KEY, rows, HEAD_SIZE), f32),
            pltpu.VMEM((2, rows, HEAD_SIZE), f32),
            pltpu.VMEM((rows, HEAD_SIZE), f32),
            pltpu.VMEM((PER_KEY * SAMPLES, context), f32),
            pltpu.VMEM((size, pairs, 2 * SAMPLES, mixed_cols), bf16),
            pltpu.VMEM((2, size, rows // 2, features), Y_TYPE),
            pltpu.VMEM((2, size, rows // 2, features), Y_TYPE),
            pltpu.VMEM((2, rows // 2, features), f32),
            pltpu.VMEM((2, rows // 2, features), bf16),
            pltpu.VMEM((2, rows // 2, features), bf16),
            dma((6,)),
            dma((size,)), dma((size,)), dma((size,)), dma((size,)),
            dma((size,)), dma((size,)),
            dma((2, size)), dma((2, size)), dma((2, size)), dma((2, size)),
            dma((size,)), dma((size,)), dma((size,)), dma((size,)),
            dma((2, 2, size)), dma((2, 2, size)),
            dma((pairs, size)), dma((pairs, size)),
            dma((2, size)), dma((2, size)),
            dma((2,)), dma((2,)),
        ],
        compiler_params=pltpu.CompilerParams(
            collective_id=0, has_side_effects=True, vmem_limit_bytes=56 * 1024 * 1024
        ),
        name="layer",
    )(
        hidden,
        query_key_value_weight,
        w_out.T,
        k_cache.reshape(prompts, context, HEAD_SIZE),
        value_cache.reshape(prompts, context, HEAD_SIZE),
        lengths.reshape(1, rows),
        assign.reshape(1, rows),
        jnp.asarray(freq),
    )
    return pl.pallas_call(
        restore_kernel,
        out_shape=jax.ShapeDtypeStruct((rows, features), bf16),
        in_specs=[vmem, vmem],
        out_specs=vmem,
        name="restore",
    )(finished, assign.reshape(1, rows))


def solution(mesh):
    return jax.shard_map(
        functools.partial(local, mesh.shape["tp"]),
        mesh=mesh,
        in_specs=(
            P("grp", "tp"),
            P(("grp", "tp"), None),
            P(None, ("grp", "tp")),
            P("grp", None, "tp", None),
            P("grp", None, "tp", None),
            P("grp"),
            P("grp"),
        ),
        out_specs=P("grp", "tp"),
        check_vma=False,
    )
```
